32 devices in a mesh: dp: 4 (over y, x), expert: 8 (over z, core).
Axes of the slice: x: 2, y: 2, z: 4, core: 2. Of those that a mesh axis runs over, the one named last changes fastest.
Arguments:
- tokens: bfloat16 [4096, 2048], P(('dp', 'expert')), may hold values from -6 to 6
- cotangent: bfloat16 [4096, 2048], P(('dp', 'expert')), may hold values from -3 to 3
- routes: int32 [4096, 1], P(('dp', 'expert')), may hold values from 0 to 7, as said below
- gate_fixed: int32 [4096, 1], P(('dp', 'expert')), may hold values from 8192 to 65535
- w_gate: bfloat16 [8, 2048, 768], P('expert', 'dp'), may hold values from -0.125 to 0.125
- w_up: bfloat16 [8, 2048, 768], P('expert', 'dp'), may hold values from -0.125 to 0.125
- w_down: bfloat16 [8, 768, 2048], P('expert', None, 'dp'), may hold values from -0.21875 to 0.21875
Outputs:
- mixed: bfloat16 [4096, 2048], P(('dp', 'expert'))
- grad_tokens: bfloat16 [4096, 2048], P(('dp', 'expert'))
- grad_w_gate: bfloat16 [8, 2048, 768], P('expert', 'dp')
- grad_w_up: bfloat16 [8, 2048, 768], P('expert', 'dp')
- grad_w_down: bfloat16 [8, 768, 2048], P('expert', None, 'dp')
The draws below stay inside these ranges and needn't reach their ends.
Inputs may be any that keep to these rules, and one draw needn't show every extreme that they name: `routes`: each token names one expert. Among the tokens of one device no expert is named more than 24 times, and some experts are named exactly 24 times by the tokens of every device.
All inputs are finite; a program needn't handle non-finite values.
Results may differ from the reference program's by a relative error of at most 0.0058.
Values may be sent and summed in bfloat16 or wider, within the bound.
No kernel may reach another device: no remote copies, remote signals or barrier semaphores. Data moves between devices by JAX's collectives and lax.ppermute only.
A program may use at most 64 MiB of HBM per device.

```python
import jax
import jax.numpy as jnp
from jax import lax

D = 2048
FF = 768
TOP = 1
TOK_DEV = 128
EXPERTS = 8
CAP = 24
TOKENS = 4096


def draw_routes(key, part):
    blocks = TOKENS // TOK_DEV
    slot_total = TOK_DEV * TOP
    half_load = slot_total // (2 * EXPERTS)
    groups = EXPERTS // 4
    key_order, key_share, key_place = jax.random.split(jax.random.fold_in(key, 7), 3)
    ranked = jax.random.permutation(key_order, EXPERTS).astype(jnp.int32)
    scores = jax.random.randint(key_share, (blocks, groups, 3), 0, 1 << 16) * 4 + jnp.arange(3, dtype=jnp.int32)
    picks = jnp.argsort(scores, axis=2)
    others = jnp.array([2, 2, 1], jnp.int32)[picks]
    leaders = jnp.full((blocks, groups, 1), 3, jnp.int32)
    quota = jnp.concatenate([leaders, others], axis=2).reshape(blocks, EXPERTS) * half_load
    bounds = jnp.cumsum(quota, axis=1)
    position = jnp.arange(slot_total, dtype=jnp.int32)
    rank_of = jnp.sum((bounds[:, None, :] <= position[None, :, None]).astype(jnp.int32), axis=2)
    chosen = ranked[rank_of]
    chosen = jnp.transpose(chosen.reshape(blocks, TOP, TOK_DEV), (0, 2, 1))
    place_scores = jax.random.randint(key_place, (blocks, TOK_DEV), 0, 1 << 16) * TOK_DEV + jnp.arange(TOK_DEV, dtype=jnp.int32)
    shuffle = jnp.argsort(place_scores, axis=1)
    chosen = jnp.take_along_axis(chosen, shuffle[:, :, None], axis=1)
    return chosen.reshape(TOKENS, TOP).astype(jnp.int32)


def with_ends(values, own_key, least, top_value):
    longest = values.shape.index(max(values.shape))
    spots = []
    for shift in (0, 1):
        where = [jax.random.randint(jax.random.fold_in(own_key, axis), (), 0, length) for axis, length in enumerate(values.shape)]
        where[longest] = (where[longest] + shift) % values.shape[longest]
        spots.append(tuple(where))
    return values.at[spots[0]].set(least).at[spots[1]].set(top_value)


def levels(own_key, shape, shards, smallest, largest):
    def one(dim, parts):
        steps = jax.random.uniform(jax.random.fold_in(jax.random.fold_in(own_key, 6), dim), (parts,), jnp.float32, smallest / len(shards), largest / len(shards))
        return jnp.repeat(jnp.exp(steps), shape[dim] // parts).reshape((-1,) + (1,) * (len(shape) - dim - 1))

    level = one(*shards[0])
    for cut in shards[1:]:
        level = level * one(*cut)
    return level


def normal_values(rng, extent, scale, most, cuts=(), kind=jnp.bfloat16):
    values = jax.random.normal(rng, extent, jnp.float32) * scale
    if len(cuts) > 0:
        values = levels(rng, extent, cuts, -0.22, 0.18) * values
    return jnp.clip(values, min=-most, max=most).astype(kind)


def setup_inputs(seed: int = 0) -> dict:
    streams_of = jax.random.split(jax.random.key(seed), 8)
    return {
        "tokens": normal_values(streams_of[0], (TOKENS, D), 1.0, 6.0, ((0, 32),)),
        "cotangent": normal_values(streams_of[1], (TOKENS, D), 0.5, 3.0, ((0, 32),)),
        "routes": draw_routes(jax.random.fold_in(streams_of[7], 71), 0),
        "gate_fixed": with_ends(jax.random.randint(streams_of[3], (TOKENS, TOP), 8192, 65536), jax.random.fold_in(streams_of[3], 1), 8192, 65535).astype(jnp.int32),
        "w_gate": normal_values(streams_of[4], (EXPERTS, D, FF), D ** -0.5, 0.125, ((0, 8), (1, 4))),
        "w_up": normal_values(streams_of[5], (EXPERTS, D, FF), D ** -0.5, 0.125, ((0, 8), (1, 4))),
        "w_down": normal_values(streams_of[6], (EXPERTS, FF, D), FF ** -0.5, 0.21875, ((0, 8), (2, 4))),
    }


def slot_index(routes):
    blocks = TOKENS // TOK_DEV
    per_block = routes.reshape(blocks, TOK_DEV * TOP)
    one_hot = (per_block[:, :, None] == jnp.arange(EXPERTS, dtype=jnp.int32)[None, None, :]).astype(jnp.int32)
    earlier = jnp.cumsum(one_hot, axis=1) - one_hot
    position = jnp.sum(earlier * one_hot, axis=2)
    block_id = jnp.arange(blocks, dtype=jnp.int32)[:, None]
    return ((per_block * blocks + block_id) * CAP + position).reshape(TOKENS * TOP).astype(jnp.int32)


def reference(tokens, cotangent, routes, gate_fixed, w_gate, w_up, w_down):
    blocks = TOKENS // TOK_DEV
    all_slots = EXPERTS * blocks * CAP
    route_weight = gate_fixed.astype(jnp.float32) / 65536.0
    index = slot_index(routes)
    route_rows = (jnp.arange(TOKENS * TOP, dtype=jnp.int32) // TOP).astype(jnp.int32)
    source_row = jnp.zeros((all_slots,), jnp.int32).at[index].set(route_rows)
    occupied = jnp.zeros((all_slots,), jnp.int32).at[index].set(1)
    slot_weight = jnp.zeros((all_slots,), jnp.float32).at[index].set(route_weight.reshape(TOKENS * TOP))
    source_row = source_row.reshape(EXPERTS, blocks * CAP)
    occupied = occupied.reshape(EXPERTS, blocks * CAP)
    slot_weight = slot_weight.reshape(EXPERTS, blocks * CAP)

    def expert_pass(inputs):
        gate_w, up_w, down_w, rows_here, filled, scale_here = inputs
        keep = filled[:, None] > 0
        inputs_here = jnp.where(keep, tokens[rows_here], jnp.zeros((), tokens.dtype))
        scaled = (scale_here[:, None] * cotangent[rows_here].astype(jnp.float32)).astype(jnp.bfloat16)
        grads_here = jnp.where(keep, scaled, jnp.zeros((), scaled.dtype))
        gate_pre = jnp.dot(inputs_here, gate_w, preferred_element_type=jnp.float32)
        up_pre = jnp.dot(inputs_here, up_w, preferred_element_type=jnp.float32)
        sigmoid_gate = jax.nn.sigmoid(gate_pre)
        hidden = (gate_pre * sigmoid_gate * up_pre).astype(jnp.bfloat16)
        outputs_here = jnp.dot(hidden, down_w, preferred_element_type=jnp.float32).astype(jnp.bfloat16)
        grad_hidden = lax.dot_general(grads_here, down_w, (((1,), (1,)), ((), ())), preferred_element_type=jnp.float32)
        grad_gate = (grad_hidden * up_pre * sigmoid_gate * (1.0 + gate_pre * (1.0 - sigmoid_gate))).astype(jnp.bfloat16)
        grad_up = (grad_hidden * gate_pre * sigmoid_gate).astype(jnp.bfloat16)
        grad_inputs = (lax.dot_general(grad_gate, gate_w, (((1,), (1,)), ((), ())), preferred_element_type=jnp.float32)
                       + lax.dot_general(grad_up, up_w, (((1,), (1,)), ((), ())), preferred_element_type=jnp.float32)).astype(jnp.bfloat16)
        grad_gate_w = lax.dot_general(inputs_here, grad_gate, (((0,), (0,)), ((), ())), preferred_element_type=jnp.float32).astype(jnp.bfloat16)
        grad_up_w = lax.dot_general(inputs_here, grad_up, (((0,), (0,)), ((), ())), preferred_element_type=jnp.float32).astype(jnp.bfloat16)
        grad_down_w = lax.dot_general(hidden, grads_here, (((0,), (0,)), ((), ())), preferred_element_type=jnp.float32).astype(jnp.bfloat16)
        return outputs_here, grad_inputs, grad_gate_w, grad_up_w, grad_down_w

    slot_out, slot_grad_in, grad_w_gate, grad_w_up, grad_w_down = lax.map(
        expert_pass, (w_gate, w_up, w_down, source_row, occupied, slot_weight))
    slot_out = slot_out.reshape(all_slots, D)
    slot_grad_in = slot_grad_in.reshape(all_slots, D)
    picked = slot_out[index].reshape(TOKENS, TOP, D).astype(jnp.float32)
    mixed = jnp.sum(route_weight[:, :, None] * picked, axis=1).astype(jnp.bfloat16)
    grad_tokens = jnp.sum(slot_grad_in[index].reshape(TOKENS, TOP, D).astype(jnp.float32), axis=1).astype(jnp.bfloat16)
    return mixed, grad_tokens, grad_w_gate, grad_w_up, grad_w_down
```

```python
import jax
import jax.numpy as jnp
from jax import lax
from jax.sharding import PartitionSpec as P

BOTH = ("dp", "expert")


def contract_last(left_side, right_side):
    return lax.dot_general(
        left_side, right_side, (((1,), (1,)), ((), ())), preferred_element_type=jnp.float32
    )


def contract_first(left_side, right_side):
    return lax.dot_general(
        left_side, right_side, (((0,), (0,)), ((), ())), preferred_element_type=jnp.float32
    )


def pair_list(experts, masks):
    return [
        (replica * experts + expert, (replica ^ masks[expert % 2]) * experts + expert)
        for replica in range(4)
        for expert in range(experts)
    ]


def swap_weight(value):
    experts = lax.axis_size("expert")
    return lax.ppermute(value, BOTH, pair_list(experts, (1, 2)))


def swap_rows(value):
    experts = lax.axis_size("expert")
    return lax.ppermute(value, BOTH, pair_list(experts, (2, 1)))


def swap_expert(value, mask):
    experts = lax.axis_size("expert")
    return lax.ppermute(value, "expert", [(i, i ^ mask) for i in range(experts)])


def turn(value):
    first, second, third, last = jnp.split(value, 4, axis=-1)
    return jnp.concatenate([first, third, second, last], axis=-1)


def send_slots(slots, chips, capacity):
    width = slots.shape[-1]
    half = width // 2
    other = swap_expert(turn(slots[1]), 1)
    rows = jnp.stack([slots[0], other], axis=1).reshape(chips, 2 * capacity, width)
    far = swap_rows(rows[:, :, half:])
    near = rows[:, :, :half]
    pieces = jnp.stack([near, far], axis=1)
    got = [pieces[0]] + [swap_expert(pieces[k], 2 * k) for k in range(1, chips)]
    return jnp.stack(got, axis=0).reshape(chips * 4 * capacity, half)


def return_slots(rows, chips, capacity):
    half = rows.shape[1]
    pieces = rows.reshape(chips, 2, 2 * capacity, half)
    got = [pieces[0]] + [swap_expert(pieces[k], 2 * k) for k in range(1, chips)]
    back = jnp.stack(got, axis=0)
    far = swap_rows(back[:, 1])
    full = jnp.concatenate([back[:, 0], far], axis=2).reshape(chips, 2, capacity, 2 * half)
    other = swap_expert(turn(full[:, 1]), 1)
    return jnp.concatenate([full[:, 0], other], axis=0).reshape(
        2 * chips * capacity, 2 * half
    )


def exchange_sum(part, chips, capacity):
    width = part.shape[1]
    turned = part.astype(jnp.bfloat16).reshape(chips, 2, 2 * capacity, width)[:, ::-1]
    return part + swap_rows(turned.reshape(part.shape)).astype(jnp.float32)


def reorder(value, order):
    rows, width = value.shape
    return jnp.take(value.reshape(rows, 4, width // 4), order, axis=1).reshape(rows, width)


def body(tokens, cotangent, routes, gate_fixed, w_gate, w_up, w_down):
    tok_count, model_width = tokens.shape
    hidden_width = w_gate.shape[2]
    experts = lax.axis_size("expert")
    chips = experts // 2
    capacity = 3 * tok_count // (2 * experts)
    replica = lax.axis_index("dp")
    expert = lax.axis_index("expert")
    side = jnp.where(expert % 2 == 0, 1, 2)
    order = replica ^ jnp.stack([0 * side, side, 3 - side, 0 * side + 3])
    inverse = jnp.argsort(order)

    w_gate, w_up, w_down = w_gate[0], w_up[0], w_down[0]
    gate_w = jnp.concatenate([w_gate, swap_weight(w_gate)], axis=0)
    up_w = jnp.concatenate([w_up, swap_weight(w_up)], axis=0)
    down_w = jnp.concatenate([w_down, swap_weight(w_down)], axis=1)

    route_weight = gate_fixed.astype(jnp.float32) / 65536.0
    one_hot = (routes == jnp.arange(experts, dtype=jnp.int32)[None, :]).astype(jnp.int32)
    position = jnp.sum((jnp.cumsum(one_hot, axis=0) - one_hot) * one_hot, axis=1)
    relative = routes[:, 0] ^ expert
    slot = ((relative % 2) * chips + relative // 2) * capacity + position
    pick = (slot[:, None] == jnp.arange(experts * capacity, dtype=jnp.int32)[None, :]).astype(
        jnp.bfloat16
    )

    scaled = (route_weight * cotangent.astype(jnp.float32)).astype(jnp.bfloat16)
    shape = (2, chips, capacity, model_width)
    slots = contract_first(pick, reorder(tokens, order)).astype(jnp.bfloat16).reshape(shape)
    grad_slots = contract_first(pick, reorder(scaled, order)).astype(jnp.bfloat16).reshape(shape)
    rows = send_slots(slots, chips, capacity)
    grad_rows = send_slots(grad_slots, chips, capacity)

    gate_part = jnp.dot(rows, gate_w, preferred_element_type=jnp.float32)
    up_part = jnp.dot(rows, up_w, preferred_element_type=jnp.float32)
    gate_pre = exchange_sum(gate_part, chips, capacity)
    up_pre = exchange_sum(up_part, chips, capacity)
    grad_hidden = exchange_sum(contract_last(grad_rows, down_w), chips, capacity)
    sigmoid_gate = jax.nn.sigmoid(gate_pre)
    hidden = (gate_pre * sigmoid_gate * up_pre).astype(jnp.bfloat16)
    slot_out = jnp.dot(hidden, down_w, preferred_element_type=jnp.float32).astype(jnp.bfloat16)
    returned = return_slots(slot_out, chips, capacity)
    grad_gate = (
        grad_hidden * up_pre * sigmoid_gate * (1.0 + gate_pre * (1.0 - sigmoid_gate))
    ).astype(jnp.bfloat16)
    grad_up = (grad_hidden * gate_pre * sigmoid_gate).astype(jnp.bfloat16)
    slot_grad_in = (contract_last(grad_gate, gate_w) + contract_last(grad_up, up_w)).astype(
        jnp.bfloat16
    )
    grad_returned = return_slots(slot_grad_in, chips, capacity)

    part = model_width // 4

    def share(pair_sum, axis):
        own, far = jnp.split(pair_sum, 2, axis=axis)
        got = swap_weight(far.astype(jnp.bfloat16)).astype(jnp.float32)
        return (own + got).astype(jnp.bfloat16)[None]

    grad_w_gate = share(contract_first(rows, grad_gate), 0)
    grad_w_up = share(contract_first(rows, grad_up), 0)
    grad_w_down = share(contract_first(hidden, grad_rows), 1)

    picked = jnp.dot(pick, returned, preferred_element_type=jnp.float32)
    mixed = reorder((route_weight * picked).astype(jnp.bfloat16), inverse)
    grad_picked = jnp.dot(pick, grad_returned, preferred_element_type=jnp.float32)
    grad_tokens = reorder(grad_picked.astype(jnp.bfloat16), inverse)
    return (mixed, grad_tokens, grad_w_gate, grad_w_up, grad_w_down)


def solution(mesh):
    return jax.shard_map(
        body,
        mesh=mesh,
        in_specs=(
            P(("dp", "expert"), None),
            P(("dp", "expert"), None),
            P(("dp", "expert"), None),
            P(("dp", "expert"), None),
            P("expert", "dp", None),
            P("expert", "dp", None),
            P("expert", None, "dp"),
        ),
        out_specs=(
            P(("dp", "expert"), None),
            P(("dp", "expert"), None),
            P("expert", "dp", None),
            P("expert", "dp", None),
            P("expert", None, "dp"),
        ),
        check_vma=False,
    )
```

```python
import functools

import jax
import jax.numpy as jnp
from jax import lax
from jax.experimental import pallas as pl
from jax.experimental.pallas import tpu as pltpu
from jax.sharding import PartitionSpec as P

BOTH = ("dp", "expert")
VMEM_BYTES = 40 * 2**20
F32 = jnp.float32
BF16 = jnp.bfloat16


def contract_last(left_side, right_side):
    return lax.dot_general(
        left_side, right_side, (((1,), (1,)), ((), ())), preferred_element_type=F32
    )


def contract_first(left_side, right_side):
    return lax.dot_general(
        left_side, right_side, (((0,), (0,)), ((), ())), preferred_element_type=F32
    )


def plain_dot(left_side, right_side):
    return jnp.dot(left_side, right_side, preferred_element_type=F32)


def pair_list(experts, masks):
    return [
        (replica * experts + expert, (replica ^ masks[expert % 2]) * experts + expert)
        for replica in range(4)
        for expert in range(experts)
    ]


def swap_weight(value):
    return lax.ppermute(value, BOTH, pair_list(lax.axis_size("expert"), (1, 2)))


def swap_rows(value):
    return lax.ppermute(value, BOTH, pair_list(lax.axis_size("expert"), (2, 1)))


def swap_expert(value, mask):
    experts = lax.axis_size("expert")
    return lax.ppermute(value, "expert", [(i, i ^ mask) for i in range(experts)])


def offset(expert, j):
    side = 1 + (expert & 1)
    return (0, side, 3 - side, 3)[j]


def after(value, *earlier):
    return lax.optimization_barrier((value,) + earlier)[0]


def params(limit=VMEM_BYTES):
    return pltpu.CompilerParams(vmem_limit_bytes=limit)


def cost(microseconds):
    return pl.CostEstimate(
        flops=int(microseconds * 1e9), bytes_accessed=int(microseconds * 3e6), transcendentals=0
    )


def whole(shape):
    return pl.BlockSpec(shape, lambda *_: (0,) * len(shape))


def slot_kernel(
    experts, capacity, tok, cot, route, fixed, gate, up, down,
    slots, grads, pick, weight, packed,
):
    strip = packed.shape[1]
    first = 0
    for source in (gate, up, down):
        count = source.shape[1]
        for j in range(source.shape[2] // strip):
            packed[pl.ds(first, count), :] = source[0, :, j * strip : (j + 1) * strip]
            first += count
    replica, expert = lax.axis_index("dp"), lax.axis_index("expert")
    chips = experts // 2
    tokens, width = tok.shape
    block = width // 4
    half_rows = chips * capacity
    routes = route[...]
    expert_row = lax.broadcasted_iota(jnp.int32, (experts, tokens), 0)
    one_hot = jnp.where(expert_row == routes, 1.0, 0.0)
    earlier = jnp.where(
        lax.broadcasted_iota(jnp.int32, (tokens, tokens), 0)
        < lax.broadcasted_iota(jnp.int32, (tokens, tokens), 1),
        1.0,
        0.0,
    )
    before = plain_dot(one_hot.astype(BF16), earlier.astype(BF16))
    position = jnp.sum(before * one_hot, axis=0, keepdims=True).astype(jnp.int32)
    relative = routes ^ expert
    slot = ((relative & 1) * chips + (relative >> 1)) * capacity + position
    rows = experts * capacity
    chosen = jnp.where(lax.broadcasted_iota(jnp.int32, (rows, tokens), 0) == slot, 1.0, 0.0)
    route_weight = fixed[...].astype(F32) / 65536.0
    slot_weight = jnp.sum(chosen * route_weight, axis=1, keepdims=True)
    pick[...] = jnp.transpose(chosen).astype(BF16)
    weight[...] = jnp.transpose(jnp.broadcast_to(route_weight, (tokens, tokens)))
    chosen = chosen.astype(BF16)
    for core in range(2):
        part = chosen[core * half_rows : (core + 1) * half_rows]
        scale = slot_weight[core * half_rows : (core + 1) * half_rows]
        for j in range(4):
            start = pl.multiple_of((replica ^ offset(expert + core, j)) * block, block)
            out = pl.ds((j % 2) * block, block)
            source = tok[:, pl.ds(start, block)]
            slots[core, j // 2, :, out] = plain_dot(part, source).astype(BF16)
            source = cot[:, pl.ds(start, block)]
            grads[core, j // 2, :, out] = (scale * plain_dot(part, source)).astype(BF16)


def make_slots(tokens, cotangent, routes, gate_fixed, weights, experts, capacity, strip):
    count, width = tokens.shape
    half_rows = experts * capacity // 2
    slot_shape = jax.ShapeDtypeStruct((2, 2, half_rows, width // 2), BF16)
    strips = [(value.shape[1], value.shape[2] // strip) for value in weights]
    packed_rows = sum(rows * n for rows, n in strips)
    return pl.pallas_call(
        functools.partial(slot_kernel, experts, capacity),
        out_shape=[
            slot_shape,
            slot_shape,
            jax.ShapeDtypeStruct((count, experts * capacity), BF16),
            jax.ShapeDtypeStruct((count, count), F32),
            jax.ShapeDtypeStruct((packed_rows, strip), BF16),
        ],
        compiler_params=params(60 * 2**20),
        cost_estimate=cost(2),
        name="make_slots",
    )(tokens, cotangent, routes.reshape(1, count), gate_fixed.reshape(1, count), *weights)


def gather_rows(pieces, out):
    rows = out.shape[0] // 2
    step = pieces[0].shape[1]
    for k, piece in enumerate(pieces):
        out[pl.ds(k * step, step), :] = piece[0]
        out[pl.ds(rows + k * step, step), :] = piece[1]


def spread_rows(value, pieces):
    rows = value.shape[0] // 2
    count, _, step, _ = pieces.shape
    for k in range(count):
        pieces[k, 0] = value[k * step : (k + 1) * step].astype(BF16)
        pieces[k, 1] = value[rows + k * step : rows + (k + 1) * step].astype(BF16)


def add_swapped(own, got):
    rows = own.shape[0] // 2
    return own + jnp.concatenate([got[rows:], got[:rows]], axis=0).astype(F32)


def gate_up_kernel(count, *refs):
    pieces, (gate, up, far_gate, far_up, rows, own, send) = refs[:count], refs[count:]

    @pl.when(pl.program_id(0) == 0)
    def _():
        gather_rows(pieces, rows)

    block = gate.shape[1]
    near_x, far_x = rows[:, :block], rows[:, block:]
    for k, (near_w, far_w) in enumerate(((gate, far_gate), (up, far_up))):
        part = plain_dot(near_x, near_w[0]) + plain_dot(far_x, far_w[...])
        own[k] = part
        send[k] = part.astype(BF16)


def gate_up_parts(pieces, w_gate, w_up, far_w, tile):
    _, step, half = pieces[0].shape
    rows = 2 * step * len(pieces)
    _, block, hidden = w_gate.shape
    near = pl.BlockSpec((1, block, tile), lambda j: (0, 0, j))
    part = pl.BlockSpec((2, rows, tile), lambda j: (0, 0, j))
    return pl.pallas_call(
        functools.partial(gate_up_kernel, len(pieces)),
        grid=(hidden // tile,),
        in_specs=[whole(pieces[0].shape)] * len(pieces)
        + [
            near,
            near,
            pl.BlockSpec((block, tile), lambda j: (j, 0)),
            pl.BlockSpec((block, tile), lambda j: (hidden // tile + j, 0)),
        ],
        out_specs=[whole((rows, half)), part, part],
        out_shape=[
            jax.ShapeDtypeStruct((rows, half), BF16),
            jax.ShapeDtypeStruct((2, rows, hidden), F32),
            jax.ShapeDtypeStruct((2, rows, hidden), BF16),
        ],
        compiler_params=params(),
        cost_estimate=cost(3),
        name="gate_up_parts",
    )(*pieces, w_gate, w_up, far_w, far_w)


def grad_hidden_kernel(count, *refs):
    pieces, (down, *far_down, rows, own, send) = refs[:count], refs[count:]

    @pl.when(pl.program_id(0) == 0)
    def _():
        gather_rows(pieces, rows)

    block = down.shape[2]
    part = contract_last(rows[:, :block], down[0])
    for k, strip in enumerate(far_down):
        width = strip.shape[1]
        part += contract_last(rows[:, block + k * width : block + (k + 1) * width], strip[...])
    own[...] = part
    send[...] = part.astype(BF16)


def down_strips(hidden, block, tile):
    first = 2 * block * hidden // tile
    return [
        pl.BlockSpec((tile, tile), lambda j, k=k: ((first + k * hidden) // tile + j, 0))
        for k in range(block // tile)
    ]


def grad_hidden_parts(pieces, w_down, far_w, tile):
    _, step, half = pieces[0].shape
    rows = 2 * step * len(pieces)
    _, hidden, block = w_down.shape
    part = pl.BlockSpec((rows, tile), lambda j: (0, j))
    strips = down_strips(hidden, block, tile)
    return pl.pallas_call(
        functools.partial(grad_hidden_kernel, len(pieces)),
        grid=(hidden // tile,),
        in_specs=[whole(pieces[0].shape)] * len(pieces)
        + [
            pl.BlockSpec((1, tile, block), lambda j: (0, j, 0)),
        ]
        + strips,
        out_specs=[whole((rows, half)), part, part],
        out_shape=[
            jax.ShapeDtypeStruct((rows, half), BF16),
            jax.ShapeDtypeStruct((rows, hidden), F32),
            jax.ShapeDtypeStruct((rows, hidden), BF16),
        ],
        compiler_params=params(),
        cost_estimate=cost(100),
        name="grad_hidden_parts",
    )(*pieces, w_down, *[far_w] * len(strips))


def slot_out_kernel(own, got, down, *refs):
    *far_down, hidden, out, total = refs
    step = pl.program_id(0)
    block = down.shape[2]
    gate_pre = add_swapped(own[0], got[0])
    up_pre = add_swapped(own[1], got[1])
    value = (gate_pre * jax.nn.sigmoid(gate_pre) * up_pre).astype(BF16)
    hidden[...] = value

    @pl.when(step == 0)
    def _():
        total[...] = jnp.zeros_like(total)

    total[:, :block] += plain_dot(value, down[0])
    for k, strip in enumerate(far_down):
        width = strip.shape[1]
        total[:, block + k * width : block + (k + 1) * width] += plain_dot(value, strip[...])

    @pl.when(step == pl.num_programs(0) - 1)
    def _():
        spread_rows(total[...], out)


def slot_out_parts(own, got, w_down, far_w, tile, count):
    _, rows, hidden = own.shape
    block = w_down.shape[2]
    part = pl.BlockSpec((2, rows, tile), lambda j: (0, 0, j))
    out_shape = (count, 2, rows // (2 * count), 2 * block)
    strips = down_strips(hidden, block, tile)
    return pl.pallas_call(
        slot_out_kernel,
        grid=(hidden // tile,),
        in_specs=[
            part,
            part,
            pl.BlockSpec((1, tile, block), lambda j: (0, j, 0)),
        ]
        + strips,
        out_specs=[pl.BlockSpec((rows, tile), lambda j: (0, j)), whole(out_shape)],
        out_shape=[
            jax.ShapeDtypeStruct((rows, hidden), BF16),
            jax.ShapeDtypeStruct(out_shape, BF16),
        ],
        scratch_shapes=[pltpu.VMEM((rows, 2 * block), F32)],
        compiler_params=params(),
        cost_estimate=cost(3),
        name="slot_out",
    )(own, got, w_down, *[far_w] * len(strips))


def slot_grad_kernel(
    own, got, own_grad, got_grad, gate, up, far_gate, far_up, rows, grad_rows, hidden,
    grads, out, far_grads, far_down, total,
):
    step = pl.program_id(0)
    block = gate.shape[1]
    gate_pre = add_swapped(own[0], got[0])
    up_pre = add_swapped(own[1], got[1])
    grad_hidden = add_swapped(own_grad[...], got_grad[...])
    sigmoid_gate = jax.nn.sigmoid(gate_pre)
    grad_gate = (
        grad_hidden * up_pre * sigmoid_gate * (1.0 + gate_pre * (1.0 - sigmoid_gate))
    ).astype(BF16)
    grad_up = (grad_hidden * gate_pre * sigmoid_gate).astype(BF16)
    grads[0] = grad_gate
    grads[1] = grad_up
    far_grads[0] = contract_first(rows[:, block:], grad_gate).astype(BF16)
    far_grads[1] = contract_first(rows[:, block:], grad_up).astype(BF16)
    far_down[...] = contract_first(hidden[...], grad_rows[:, block:]).astype(BF16)

    @pl.when(step == 0)
    def _():
        total[...] = jnp.zeros_like(total)

    total[:, :block] += contract_last(grad_gate, gate[0]) + contract_last(grad_up, up[0])
    total[:, block:] += contract_last(grad_gate, far_gate[...]) + contract_last(
        grad_up, far_up[...]
    )

    @pl.when(step == pl.num_programs(0) - 1)
    def _():
        spread_rows(total[...], out)


def slot_grad_parts(own, got, own_grad, got_grad, w_gate, w_up, far_w, x, y, h, tile, count):
    _, rows, hidden = own.shape
    block = w_gate.shape[1]
    part = pl.BlockSpec((2, rows, tile), lambda j: (0, 0, j))
    near = pl.BlockSpec((1, block, tile), lambda j: (0, 0, j))
    grad_part = pl.BlockSpec((rows, tile), lambda j: (0, j))
    out_shape = (count, 2, rows // (2 * count), 2 * block)
    return pl.pallas_call(
        slot_grad_kernel,
        grid=(hidden // tile,),
        in_specs=[
            part,
            part,
            grad_part,
            grad_part,
            near,
            near,
            pl.BlockSpec((block, tile), lambda j: (j, 0)),
            pl.BlockSpec((block, tile), lambda j: (hidden // tile + j, 0)),
            whole(x.shape),
            whole(y.shape),
            grad_part,
        ],
        out_specs=[
            part,
            whole(out_shape),
            pl.BlockSpec((2, block, tile), lambda j: (0, 0, j)),
            pl.BlockSpec((tile, block), lambda j: (j, 0)),
        ],
        out_shape=[
            jax.ShapeDtypeStruct((2, rows, hidden), BF16),
            jax.ShapeDtypeStruct(out_shape, BF16),
            jax.ShapeDtypeStruct((2, block, hidden), BF16),
            jax.ShapeDtypeStruct((hidden, block), BF16),
        ],
        scratch_shapes=[pltpu.VMEM((rows, 2 * block), F32)],
        compiler_params=params(),
        cost_estimate=cost(100),
        name="slot_grad",
    )(own, got, own_grad, got_grad, w_gate, w_up, far_w, far_w, x, y, h)


def unslot_kernel(weighted, pick, weight, near, far, other, out):
    half_rows, half = near.shape
    block = half // 2
    replica, expert = lax.axis_index("dp"), lax.axis_index("expert")
    for j in range(4):
        start = pl.multiple_of((replica ^ offset(expert, j)) * block, block)
        own = (near if j < 2 else far)[:, pl.ds((j % 2) * block, block)]
        k = (0, 2, 1, 3)[j]
        rest = other[k // 2, :, pl.ds((k % 2) * block, block)]
        value = plain_dot(pick[:, :half_rows], own) + plain_dot(pick[:, half_rows:], rest)
        if weighted:
            value = weight[:, :1] * value
        out[:, pl.ds(start, block)] = value.astype(BF16)


def unslot(pick, weight, near, far, other, weighted):
    count = pick.shape[0]
    half_rows, half = near.shape
    return pl.pallas_call(
        functools.partial(unslot_kernel, weighted),
        out_shape=jax.ShapeDtypeStruct((count, 2 * half), BF16),
        compiler_params=params(),
        cost_estimate=cost(2),
        name="unslot",
    )(pick, weight, near, far, other)


def swap_chips(pieces, earlier):
    got = [pieces[0]]
    for k in range(1, len(pieces)):
        value = pieces[k] if earlier is None else after(pieces[k], earlier[k])
        got.append(swap_expert(value, 2 * k))
    return got


def send_slots(slots, chips, capacity, earlier_far, earlier):
    half = slots.shape[-1]
    other = swap_expert(slots[1], 1)
    far = jnp.stack([slots[0, 1], other[1]], axis=0)
    far = swap_rows(far if earlier_far is None else after(far, earlier_far))
    shape = (chips, 1, capacity, half)
    near = jnp.concatenate([slots[0, 0].reshape(shape), other[0].reshape(shape)], axis=1)
    both = jnp.concatenate([far[0].reshape(shape), far[1].reshape(shape)], axis=1)
    shape = (2 * capacity, half)
    pieces = [
        jnp.stack([near[k].reshape(shape), both[k].reshape(shape)], axis=0) for k in range(chips)
    ]
    return far, swap_chips(pieces, earlier)


def return_slots(got, chips, capacity, before_rows, before_core):
    half = got[0].shape[-1]
    far = swap_rows(after(jnp.stack([piece[1] for piece in got], axis=0), *before_rows))
    near = jnp.stack([piece[0] for piece in got], axis=0)
    shape = (chips, 2, capacity, half)
    near, far = near.reshape(shape), far.reshape(shape)
    rows = chips * capacity
    other = jnp.stack([near[:, 1].reshape(rows, half), far[:, 1].reshape(rows, half)], axis=0)
    other = swap_expert(after(other, *before_core), 1)
    return near[:, 0].reshape(rows, half), far[:, 0].reshape(rows, half), other


def body(tokens, cotangent, routes, gate_fixed, w_gate, w_up, w_down):
    tok_count, model_width = tokens.shape
    hidden_width = w_gate.shape[2]
    experts = lax.axis_size("expert")
    chips = experts // 2
    capacity = 3 * tok_count // (2 * experts)
    block = model_width // 4
    tile = 256 if hidden_width % 256 == 0 else hidden_width
    slots, grad_slots, pick, weight, packed = make_slots(
        tokens, cotangent, routes, gate_fixed, (w_gate, w_up, w_down), experts, capacity, tile
    )
    far_w = swap_weight(packed)
    far, got_pieces = send_slots(slots, chips, capacity, None, None)
    _, got_grad_pieces = send_slots(grad_slots, chips, capacity, far, got_pieces)
    aligned = (2 * capacity) % 16 == 0

    def merged(pieces):
        return pieces if aligned else [jnp.concatenate(pieces, axis=1)]

    def split(value):
        if aligned:
            return [value[k] for k in range(chips)]
        value = value.reshape(2, chips, 2 * capacity, 2 * block)
        return [value[:, k] for k in range(chips)]

    pieces, grad_pieces = merged(got_pieces), merged(got_grad_pieces)
    rows, own, send = gate_up_parts(pieces, w_gate, w_up, far_w, tile)
    got = swap_rows(send)
    grad_rows, own_grad, send_grad = grad_hidden_parts(grad_pieces, w_down, far_w, tile)
    got_grad = swap_rows(send_grad)

    hidden, slot_out = slot_out_parts(own, got, w_down, far_w, tile, len(pieces))
    out_pieces = swap_chips(split(slot_out), None)
    grads, slot_grad, far_grads, far_down = slot_grad_parts(
        own, got, own_grad, got_grad, w_gate, w_up, far_w, rows, grad_rows, hidden, tile, len(pieces)
    )
    grad_out_pieces = swap_chips(split(slot_grad), out_pieces)

    got_far = swap_weight(far_grads)
    got_down = swap_weight(far_down)
    grad_w_gate = contract_first(rows[:, :block], grads[0]) + got_far[0].astype(F32)
    grad_w_up = contract_first(rows[:, :block], grads[1]) + got_far[1].astype(F32)
    grad_w_down = contract_first(hidden, grad_rows[:, :block]) + got_down.astype(F32)
    grad_w_gate, grad_w_up, grad_w_down = (
        value.astype(BF16)[None] for value in (grad_w_gate, grad_w_up, grad_w_down)
    )

    back = return_slots(out_pieces, chips, capacity, (), ())
    mixed = unslot(pick, weight, *back, True)
    grad_back = return_slots(
        grad_out_pieces, chips, capacity, (got_down,), (mixed, grad_w_gate, grad_w_up, grad_w_down)
    )
    grad_tokens = unslot(pick, weight, *grad_back, False)
    return (
        mixed,
        grad_tokens,
        grad_w_gate,
        grad_w_up,
        grad_w_down,
    )


def solution(mesh):
    return jax.shard_map(
        body,
        mesh=mesh,
        in_specs=(
            P(("dp", "expert"), None),
            P(("dp", "expert"), None),
            P(("dp", "expert"), None),
            P(("dp", "expert"), None),
            P("expert", "dp", None),
            P("expert", "dp", None),
            P("expert", None, "dp"),
        ),
        out_specs=(
            P(("dp", "expert"), None),
            P(("dp", "expert"), None),
            P("expert", "dp", None),
            P("expert", "dp", None),
            P("expert", None, "dp"),
        ),
        check_vma=False,
    )
```

```python
import functools

import jax
import jax.numpy as jnp
from jax import lax
from jax.experimental import pallas as pl
from jax.experimental.pallas import tpu as pltpu
from jax.sharding import PartitionSpec as P

BOTH = ("dp", "expert")
VMEM_BYTES = 40 * 2**20
F32 = jnp.float32
BF16 = jnp.bfloat16


def contract_last(left_side, right_side):
    return lax.dot_general(
        left_side, right_side, (((1,), (1,)), ((), ())), preferred_element_type=F32
    )


def contract_first(left_side, right_side):
    return lax.dot_general(
        left_side, right_side, (((0,), (0,)), ((), ())), preferred_element_type=F32
    )


def plain_dot(left_side, right_side):
    return jnp.dot(left_side, right_side, preferred_element_type=F32)


def pair_list(experts, masks):
    return [
        (replica * experts + expert, (replica ^ masks[expert % 2]) * experts + expert)
        for replica in range(4)
        for expert in range(experts)
    ]


def swap_weight(value):
    return lax.ppermute(value, BOTH, pair_list(lax.axis_size("expert"), (1, 2)))


def swap_rows(value):
    return lax.ppermute(value, BOTH, pair_list(lax.axis_size("expert"), (2, 1)))


def swap_expert(value, mask):
    experts = lax.axis_size("expert")
    return lax.ppermute(value, "expert", [(i, i ^ mask) for i in range(experts)])


def offset(expert, j):
    side = 1 + (expert & 1)
    return (0, side, 3 - side, 3)[j]


def after(value, *earlier):
    return lax.optimization_barrier((value,) + earlier)[0]


def params(limit=VMEM_BYTES):
    return pltpu.CompilerParams(vmem_limit_bytes=limit)


def cost(microseconds):
    return pl.CostEstimate(
        flops=int(microseconds * 1e9), bytes_accessed=int(microseconds * 3e6), transcendentals=0
    )


def whole(shape):
    return pl.BlockSpec(shape, lambda *_: (0,) * len(shape))


def choose(experts, capacity, route, fixed):
    chips = experts // 2
    tokens = route.shape[1]
    routes = route[...]
    expert = lax.axis_index("expert")
    expert_row = lax.broadcasted_iota(jnp.int32, (experts, tokens), 0)
    one_hot = jnp.where(expert_row == routes, 1.0, 0.0)
    earlier = jnp.where(
        lax.broadcasted_iota(jnp.int32, (tokens, tokens), 0)
        < lax.broadcasted_iota(jnp.int32, (tokens, tokens), 1),
        1.0,
        0.0,
    )
    before = plain_dot(one_hot.astype(BF16), earlier.astype(BF16))
    position = jnp.sum(before * one_hot, axis=0, keepdims=True).astype(jnp.int32)
    relative = routes ^ expert
    slot = ((relative & 1) * chips + (relative >> 1)) * capacity + position
    rows = experts * capacity
    chosen = jnp.where(lax.broadcasted_iota(jnp.int32, (rows, tokens), 0) == slot, 1.0, 0.0)
    return chosen, fixed[...].astype(F32) / 65536.0


def fill(chosen, scale, source, *outs):
    half_rows = chosen.shape[0] // 2
    block = source.shape[1] // 4
    replica, expert = lax.axis_index("dp"), lax.axis_index("expert")
    chosen = chosen.astype(BF16)
    for core, out in enumerate(outs):
        part = chosen[core * half_rows : (core + 1) * half_rows]
        for j in range(4):
            start = pl.multiple_of((replica ^ offset(expert + core, j)) * block, block)
            value = plain_dot(part, source[:, pl.ds(start, block)])
            if scale is not None:
                value = scale[core * half_rows : (core + 1) * half_rows] * value
            out[j // 2, :, pl.ds((j % 2) * block, block)] = value.astype(BF16)


def slot_kernel(experts, capacity, tok, route, fixed, own, other):
    chosen, _ = choose(experts, capacity, route, fixed)
    fill(chosen, None, tok, own, other)


def grad_kernel(experts, capacity, cot, route, fixed, own, other, pick, weight):
    chosen, route_weight = choose(experts, capacity, route, fixed)
    tokens = cot.shape[0]
    pick[...] = jnp.transpose(chosen).astype(BF16)
    weight[...] = jnp.transpose(jnp.broadcast_to(route_weight, (tokens, tokens)))
    fill(chosen, jnp.sum(chosen * route_weight, axis=1, keepdims=True), cot, own, other)


def make_slots(tokens, routes, gate_fixed, experts, capacity):
    count, width = tokens.shape
    slot_shape = jax.ShapeDtypeStruct((2, experts * capacity // 2, width // 2), BF16)
    return pl.pallas_call(
        functools.partial(slot_kernel, experts, capacity),
        out_shape=[slot_shape] * 2,
        compiler_params=params(60 * 2**20),
        cost_estimate=cost(0.01),
        name="make_slots",
    )(tokens, routes.reshape(1, count), gate_fixed.reshape(1, count))


def make_grads(cotangent, routes, gate_fixed, experts, capacity):
    count, width = cotangent.shape
    slot_shape = jax.ShapeDtypeStruct((2, experts * capacity // 2, width // 2), BF16)
    return pl.pallas_call(
        functools.partial(grad_kernel, experts, capacity),
        out_shape=[slot_shape] * 2
        + [
            jax.ShapeDtypeStruct((count, experts * capacity), BF16),
            jax.ShapeDtypeStruct((count, count), F32),
        ],
        compiler_params=params(60 * 2**20),
        cost_estimate=cost(0.01),
        name="make_grads",
    )(cotangent, routes.reshape(1, count), gate_fixed.reshape(1, count))


def gather_rows(parts, places, out):
    for part, blocks in zip(parts, places):
        step = part.shape[1]
        for i, block in enumerate(blocks):
            out[pl.ds(block * step, step), :] = part[i]


def spread_rows(value, parts, places):
    for part, blocks in zip(parts, places):
        step = part.shape[1]
        for i, block in enumerate(blocks):
            part[i] = value[block * step : (block + 1) * step].astype(BF16)


def row_count(parts):
    return sum(part.shape[0] * part.shape[1] for part in parts)


def part_shapes(rows, width, places):
    step = rows // sum(len(blocks) for blocks in places)
    return [(len(blocks), step, width) for blocks in places]


def add_swapped(own, got):
    rows = own.shape[0] // 2
    return own + jnp.concatenate([got[rows:], got[:rows]], axis=0).astype(F32)


def gate_up_kernel(places, *refs):
    count = len(places)
    parts, (gate, up, far_gate, far_up, rows, own, send) = refs[:count], refs[count:]

    @pl.when(pl.program_id(0) == 0)
    def _():
        gather_rows(parts, places, rows)

    block = gate.shape[1]
    near_x, far_x = rows[:, :block], rows[:, block:]
    for k, (near_w, far_w) in enumerate(((gate, far_gate), (up, far_up))):
        part = plain_dot(near_x, near_w[0]) + plain_dot(far_x, far_w[0])
        own[k] = part
        send[k] = part.astype(BF16)


def gate_up_parts(parts, places, w_gate, w_up, far_gate, far_up, tile):
    rows, half = row_count(parts), parts[0].shape[-1]
    _, block, hidden = w_gate.shape
    near = pl.BlockSpec((1, block, tile), lambda j: (0, 0, j))
    part = pl.BlockSpec((2, rows, tile), lambda j: (0, 0, j))
    return pl.pallas_call(
        functools.partial(gate_up_kernel, places),
        grid=(hidden // tile,),
        in_specs=[whole(part.shape) for part in parts]
        + [
            near,
            near,
            near,
            near,
        ],
        out_specs=[whole((rows, half)), part, part],
        out_shape=[
            jax.ShapeDtypeStruct((rows, half), BF16),
            jax.ShapeDtypeStruct((2, rows, hidden), F32),
            jax.ShapeDtypeStruct((2, rows, hidden), BF16),
        ],
        compiler_params=params(),
        cost_estimate=cost(0.01),
        name="gate_up_parts",
    )(*parts, w_gate, w_up, far_gate, far_up)


def grad_hidden_kernel(places, *refs):
    count = len(places)
    parts, (down, far_down, rows, own, send) = refs[:count], refs[count:]

    @pl.when(pl.program_id(0) == 0)
    def _():
        gather_rows(parts, places, rows)

    block = down.shape[2]
    part = contract_last(rows[:, :block], down[0]) + contract_last(rows[:, block:], far_down[0])
    own[...] = part
    send[...] = part.astype(BF16)


def grad_hidden_parts(parts, places, w_down, far_down, tile):
    rows, half = row_count(parts), parts[0].shape[-1]
    _, hidden, block = w_down.shape
    part = pl.BlockSpec((rows, tile), lambda j: (0, j))
    near = pl.BlockSpec((1, tile, block), lambda j: (0, j, 0))
    return pl.pallas_call(
        functools.partial(grad_hidden_kernel, places),
        grid=(hidden // tile,),
        in_specs=[whole(part.shape) for part in parts]
        + [
            near,
            near,
        ],
        out_specs=[whole((rows, half)), part, part],
        out_shape=[
            jax.ShapeDtypeStruct((rows, half), BF16),
            jax.ShapeDtypeStruct((rows, hidden), F32),
            jax.ShapeDtypeStruct((rows, hidden), BF16),
        ],
        compiler_params=params(),
        cost_estimate=cost(1),
        name="grad_hidden_parts",
    )(*parts, w_down, far_down)


def slot_out_kernel(places, own, got, down, far_down, grad_rows, hidden, far_grad, *refs):
    *out, total = refs
    step = pl.program_id(0)
    block = down.shape[2]
    gate_pre = add_swapped(own[0], got[0])
    up_pre = add_swapped(own[1], got[1])
    value = (gate_pre * jax.nn.sigmoid(gate_pre) * up_pre).astype(BF16)
    hidden[...] = value

    @pl.when(step == 0)
    def _():
        total[...] = jnp.zeros_like(total)

    total[:, :block] += plain_dot(value, down[0])
    total[:, block:] += plain_dot(value, far_down[0])
    far_grad[...] = contract_first(value, grad_rows[:, block:]).astype(BF16)

    @pl.when(step == pl.num_programs(0) - 1)
    def _():
        spread_rows(total[...], out, places)


def slot_out_parts(own, got, w_down, far_down, y, tile, places):
    _, rows, hidden = own.shape
    block = w_down.shape[2]
    part = pl.BlockSpec((2, rows, tile), lambda j: (0, 0, j))
    shapes = part_shapes(rows, 2 * block, places)
    near = pl.BlockSpec((1, tile, block), lambda j: (0, j, 0))
    return pl.pallas_call(
        functools.partial(slot_out_kernel, places),
        grid=(hidden // tile,),
        in_specs=[
            part,
            part,
            near,
            near,
            whole(y.shape),
        ],
        out_specs=[
            pl.BlockSpec((rows, tile), lambda j: (0, j)),
            pl.BlockSpec((tile, block), lambda j: (j, 0)),
        ]
        + [whole(shape) for shape in shapes],
        out_shape=[
            jax.ShapeDtypeStruct((rows, hidden), BF16),
            jax.ShapeDtypeStruct((hidden, block), BF16),
        ]
        + [jax.ShapeDtypeStruct(shape, BF16) for shape in shapes],
        scratch_shapes=[pltpu.VMEM((rows, 2 * block), F32)],
        compiler_params=params(),
        cost_estimate=cost(0.01),
        name="slot_out",
    )(own, got, w_down, far_down, y)


def slot_grad_kernel(
    places, own, got, own_grad, got_grad, gate, up, far_gate, far_up, rows,
    grads, far_grads, *refs,
):
    *out, total = refs
    step = pl.program_id(0)
    block = gate.shape[1]
    gate_pre = add_swapped(own[0], got[0])
    up_pre = add_swapped(own[1], got[1])
    grad_hidden = add_swapped(own_grad[...], got_grad[...])
    sigmoid_gate = jax.nn.sigmoid(gate_pre)
    grad_gate = (
        grad_hidden * up_pre * sigmoid_gate * (1.0 + gate_pre * (1.0 - sigmoid_gate))
    ).astype(BF16)
    grad_up = (grad_hidden * gate_pre * sigmoid_gate).astype(BF16)
    grads[0] = grad_gate
    grads[1] = grad_up
    far_grads[0] = contract_first(rows[:, block:], grad_gate).astype(BF16)
    far_grads[1] = contract_first(rows[:, block:], grad_up).astype(BF16)

    @pl.when(step == 0)
    def _():
        total[...] = jnp.zeros_like(total)

    total[:, :block] += contract_last(grad_gate, gate[0]) + contract_last(grad_up, up[0])
    total[:, block:] += contract_last(grad_gate, far_gate[0]) + contract_last(
        grad_up, far_up[0]
    )

    @pl.when(step == pl.num_programs(0) - 1)
    def _():
        spread_rows(total[...], out, places)


def slot_grad_parts(own, got, own_grad, got_grad, w_gate, w_up, far_gate, far_up, x, tile, places):
    _, rows, hidden = own.shape
    block = w_gate.shape[1]
    part = pl.BlockSpec((2, rows, tile), lambda j: (0, 0, j))
    near = pl.BlockSpec((1, block, tile), lambda j: (0, 0, j))
    grad_part = pl.BlockSpec((rows, tile), lambda j: (0, j))
    shapes = part_shapes(rows, 2 * block, places)
    return pl.pallas_call(
        functools.partial(slot_grad_kernel, places),
        grid=(hidden // tile,),
        in_specs=[
            part,
            part,
            grad_part,
            grad_part,
            near,
            near,
            near,
            near,
            whole(x.shape),
        ],
        out_specs=[
            part,
            pl.BlockSpec((2, block, tile), lambda j: (0, 0, j)),
        ]
        + [whole(shape) for shape in shapes],
        out_shape=[
            jax.ShapeDtypeStruct((2, rows, hidden), BF16),
            jax.ShapeDtypeStruct((2, block, hidden), BF16),
        ]
        + [jax.ShapeDtypeStruct(shape, BF16) for shape in shapes],
        scratch_shapes=[pltpu.VMEM((rows, 2 * block), F32)],
        compiler_params=params(),
        cost_estimate=cost(0),
        name="slot_grad",
    )(own, got, own_grad, got_grad, w_gate, w_up, far_gate, far_up, x)


def unslot_kernel(weighted, pick, weight, near, far, other, out):
    half_rows, half = near.shape
    block = half // 2
    replica, expert = lax.axis_index("dp"), lax.axis_index("expert")
    for j in range(4):
        start = pl.multiple_of((replica ^ offset(expert, j)) * block, block)
        own = (near if j < 2 else far)[:, pl.ds((j % 2) * block, block)]
        k = (0, 2, 1, 3)[j]
        rest = other[k // 2, :, pl.ds((k % 2) * block, block)]
        value = plain_dot(pick[:, :half_rows], own) + plain_dot(pick[:, half_rows:], rest)
        if weighted:
            value = weight[:, :1] * value
        out[:, pl.ds(start, block)] = value.astype(BF16)


def unslot(pick, weight, near, far, other, weighted):
    count = pick.shape[0]
    half_rows, half = near.shape
    return pl.pallas_call(
        functools.partial(unslot_kernel, weighted),
        out_shape=jax.ShapeDtypeStruct((count, 2 * half), BF16),
        compiler_params=params(),
        cost_estimate=cost(0.01),
        name="unslot",
    )(pick, weight, near, far, other)


def swap_chips(parts, chips, *earlier):
    got = list(parts)
    for first in range(0, len(parts), chips):
        for k in range(1, chips):
            got[first + k] = swap_expert(after(parts[first + k], *earlier), 2 * k)
    return got


def send_slots(slots, others, chips, capacity, apart, before_rows, before_near, before_far):
    half = slots.shape[-1]
    other = swap_expert(others, 1)
    far = swap_rows(after(jnp.stack([slots[1], other[1]], axis=0), *before_rows))

    def by_chip(own, rest):
        shape = (chips, 1, capacity, half)
        both = jnp.concatenate([own.reshape(shape), rest.reshape(shape)], axis=1)
        return [both[k].reshape(1, 2 * capacity, half) for k in range(chips)]

    near_parts, far_parts = by_chip(slots[0], other[0]), by_chip(far[0], far[1])
    if apart:
        near_parts = swap_chips(near_parts, chips, *before_near)
        return far, near_parts + swap_chips(far_parts, chips, *before_far)
    parts = [jnp.concatenate(pair, axis=0) for pair in zip(near_parts, far_parts)]
    return far, swap_chips(parts, chips, *before_near)


def return_slots(parts, chips, capacity, before_rows, before_core):
    half = parts[0].shape[-1]
    if len(parts) == chips:
        parts = [part[:1] for part in parts] + [part[1:] for part in parts]
    shape = (chips, 2, capacity, half)
    far = swap_rows(after(jnp.concatenate(parts[chips:], axis=0), *before_rows)).reshape(shape)
    near = jnp.concatenate(parts[:chips], axis=0).reshape(shape)
    rows = chips * capacity
    other = jnp.stack([near[:, 1].reshape(rows, half), far[:, 1].reshape(rows, half)], axis=0)
    other = swap_expert(after(other, *before_core), 1)
    return near[:, 0].reshape(rows, half), far[:, 0].reshape(rows, half), other


def body(tokens, cotangent, routes, gate_fixed, w_gate, w_up, w_down):
    tok_count, model_width = tokens.shape
    hidden_width = w_gate.shape[2]
    experts = lax.axis_size("expert")
    chips = experts // 2
    capacity = 3 * tok_count // (2 * experts)
    block = model_width // 4
    tile = 256 if hidden_width % 256 == 0 else hidden_width
    far_gate = swap_weight(w_gate)
    slots, others = make_slots(tokens, routes, gate_fixed, experts, capacity)
    grad_slots, grad_others, pick, weight = make_grads(
        cotangent, routes, gate_fixed, experts, capacity
    )
    far, got_parts = send_slots(
        slots, others, chips, capacity, True, (), (), ()
    )
    far_up = swap_weight(w_up)
    far_down = swap_weight(after(w_down, *(far,)))
    grad_far, got_grad_parts = send_slots(
        grad_slots, grad_others, chips, capacity, False, (far_up,), got_parts, got_parts
    )
    if (2 * capacity) % 16 == 0:
        apart = tuple((k,) for k in range(2 * chips))
        paired = tuple((k, k + chips) for k in range(chips))
    else:
        apart = paired = ((0,),)

    def joined(parts):
        if apart != paired:
            return parts
        if len(parts) == chips:
            parts = [part[:1] for part in parts] + [part[1:] for part in parts]
        return [jnp.concatenate(parts, axis=1)]

    def cut(parts):
        if apart != paired:
            return parts
        return jnp.split(parts[0], 2 * chips, axis=1)

    rows, own, send = gate_up_parts(
        joined(got_parts), apart, w_gate, w_up, far_gate, far_up, tile
    )
    got = swap_rows(send)
    grad_rows, own_grad, send_grad = grad_hidden_parts(
        joined(got_grad_parts), paired, after(w_down, *(send,)), far_down, tile
    )
    got_grad = swap_rows(send_grad)

    hidden, far_grad_down, *slot_out = slot_out_parts(
        own, got, w_down, far_down, grad_rows, tile, paired
    )
    out_parts = swap_chips(cut(slot_out), chips)
    sent = [part for k, part in enumerate(out_parts) if k % chips]
    got_down = swap_weight(far_grad_down)
    grads, far_grads, *slot_grad = slot_grad_parts(
        own,
        got,
        own_grad,
        after(got_grad, *(hidden,)),
        w_gate,
        w_up,
        far_gate,
        far_up,
        rows,
        tile,
        paired,
    )
    grad_out_parts = swap_chips(cut(slot_grad), chips, *sent)
    got_far = swap_weight(after(far_grads, *sent[:1]))

    grad_w_gate = contract_first(rows[:, :block], grads[0]) + got_far[0].astype(F32)
    grad_w_up = contract_first(rows[:, :block], grads[1]) + got_far[1].astype(F32)
    grad_w_down = contract_first(hidden, grad_rows[:, :block]) + got_down.astype(F32)
    grad_w_gate, grad_w_up, grad_w_down = (
        value.astype(BF16)[None] for value in (grad_w_gate, grad_w_up, grad_w_down)
    )

    back = return_slots(out_parts, chips, capacity, (slot_grad[0],), ())
    mixed = unslot(pick, weight, *back, True)
    grad_back = return_slots(grad_out_parts, chips, capacity, (got_down,), (mixed, grad_w_gate, grad_w_up, grad_w_down))
    grad_tokens = unslot(pick, weight, *grad_back, False)
    return (
        mixed,
        grad_tokens,
        grad_w_gate,
        grad_w_up,
        grad_w_down,
    )


def solution(mesh):
    return jax.shard_map(
        body,
        mesh=mesh,
        in_specs=(
            P(("dp", "expert"), None),
            P(("dp", "expert"), None),
            P(("dp", "expert"), None),
            P(("dp", "expert"), None),
            P("expert", "dp", None),
            P("expert", "dp", None),
            P("expert", None, "dp"),
        ),
        out_specs=(
            P(("dp", "expert"), None),
            P(("dp", "expert"), None),
            P("expert", "dp", None),
            P("expert", "dp", None),
            P("expert", None, "dp"),
        ),
        check_vma=False,
    )
```

```python
import functools

import jax
import jax.numpy as jnp
from jax import lax
from jax.experimental import pallas as pl
from jax.experimental.pallas import tpu as pltpu
from jax.sharding import PartitionSpec as P

BOTH = ("dp", "expert")
VMEM_BYTES = 40 * 2**20
F32 = jnp.float32
BF16 = jnp.bfloat16


def contract_last(left_side, right_side):
    return lax.dot_general(
        left_side, right_side, (((1,), (1,)), ((), ())), preferred_element_type=F32
    )


def contract_first(left_side, right_side):
    return lax.dot_general(
        left_side, right_side, (((0,), (0,)), ((), ())), preferred_element_type=F32
    )


def plain_dot(left_side, right_side):
    return jnp.dot(left_side, right_side, preferred_element_type=F32)


def pair_list(experts, masks):
    return [
        (replica * experts + expert, (replica ^ masks[expert % 2]) * experts + expert)
        for replica in range(4)
        for expert in range(experts)
    ]


def swap_weight(value):
    return lax.ppermute(value, BOTH, pair_list(lax.axis_size("expert"), (1, 2)))


def swap_rows(value):
    return lax.ppermute(value, BOTH, pair_list(lax.axis_size("expert"), (2, 1)))


def swap_expert(value, mask):
    experts = lax.axis_size("expert")
    return lax.ppermute(value, "expert", [(i, i ^ mask) for i in range(experts)])


def offset(expert, j):
    side = 1 + (expert & 1)
    return (0, side, 3 - side, 3)[j]


def after(value, *earlier):
    return lax.optimization_barrier((value,) + earlier)[0]


def params(limit=VMEM_BYTES):
    return pltpu.CompilerParams(vmem_limit_bytes=limit)


def cost(microseconds):
    return pl.CostEstimate(
        flops=int(microseconds * 1e9), bytes_accessed=int(microseconds * 3e6), transcendentals=0
    )


def whole(shape):
    return pl.BlockSpec(shape, lambda *_: (0,) * len(shape))


def choose(experts, capacity, route, fixed):
    chips = experts // 2
    tokens = route.shape[1]
    routes = route[...]
    expert = lax.axis_index("expert")
    expert_row = lax.broadcasted_iota(jnp.int32, (experts, tokens), 0)
    one_hot = jnp.where(expert_row == routes, 1.0, 0.0)
    earlier = jnp.where(
        lax.broadcasted_iota(jnp.int32, (tokens, tokens), 0)
        < lax.broadcasted_iota(jnp.int32, (tokens, tokens), 1),
        1.0,
        0.0,
    )
    before = plain_dot(one_hot.astype(BF16), earlier.astype(BF16))
    position = jnp.sum(before * one_hot, axis=0, keepdims=True).astype(jnp.int32)
    relative = routes ^ expert
    slot = ((relative & 1) * chips + (relative >> 1)) * capacity + position
    rows = experts * capacity
    chosen = jnp.where(lax.broadcasted_iota(jnp.int32, (rows, tokens), 0) == slot, 1.0, 0.0)
    return chosen, fixed[...].astype(F32) / 65536.0


def fill(chosen, scale, source, *outs):
    half_rows = chosen.shape[0] // 2
    block = source.shape[1] // 4
    replica, expert = lax.axis_index("dp"), lax.axis_index("expert")
    chosen = chosen.astype(BF16)
    for core, out in enumerate(outs):
        part = chosen[core * half_rows : (core + 1) * half_rows]
        for j in range(4):
            start = pl.multiple_of((replica ^ offset(expert + core, j)) * block, block)
            value = plain_dot(part, source[:, pl.ds(start, block)])
            if scale is not None:
                value = scale[core * half_rows : (core + 1) * half_rows] * value
            out[j // 2, :, pl.ds((j % 2) * block, block)] = value.astype(BF16)


def slot_kernel(experts, capacity, tok, route, fixed, own, other):
    chosen, _ = choose(experts, capacity, route, fixed)
    fill(chosen, None, tok, own, other)


def grad_kernel(experts, capacity, cot, route, fixed, own, other, pick, weight):
    chosen, route_weight = choose(experts, capacity, route, fixed)
    tokens = cot.shape[0]
    pick[...] = jnp.transpose(chosen).astype(BF16)
    weight[...] = jnp.transpose(jnp.broadcast_to(route_weight, (tokens, tokens)))
    fill(chosen, jnp.sum(chosen * route_weight, axis=1, keepdims=True), cot, own, other)


def make_slots(tokens, routes, gate_fixed, experts, capacity):
    count, width = tokens.shape
    slot_shape = jax.ShapeDtypeStruct((2, experts * capacity // 2, width // 2), BF16)
    return pl.pallas_call(
        functools.partial(slot_kernel, experts, capacity),
        out_shape=[slot_shape] * 2,
        compiler_params=params(60 * 2**20),
        cost_estimate=cost(0.01),
        name="make_slots",
    )(tokens, routes.reshape(1, count), gate_fixed.reshape(1, count))


def make_grads(cotangent, routes, gate_fixed, experts, capacity):
    count, width = cotangent.shape
    slot_shape = jax.ShapeDtypeStruct((2, experts * capacity // 2, width // 2), BF16)
    return pl.pallas_call(
        functools.partial(grad_kernel, experts, capacity),
        out_shape=[slot_shape] * 2
        + [
            jax.ShapeDtypeStruct((count, experts * capacity), BF16),
            jax.ShapeDtypeStruct((count, count), F32),
        ],
        compiler_params=params(60 * 2**20),
        cost_estimate=cost(0.01),
        name="make_grads",
    )(cotangent, routes.reshape(1, count), gate_fixed.reshape(1, count))


def gather_rows(parts, places, out):
    for part, blocks in zip(parts, places):
        step = part.shape[1]
        for i, block in enumerate(blocks):
            out[pl.ds(block * step, step), :] = part[i]


def spread_rows(value, parts, places):
    for part, blocks in zip(parts, places):
        step = part.shape[1]
        for i, block in enumerate(blocks):
            part[i] = value[block * step : (block + 1) * step].astype(BF16)


def row_count(parts):
    return sum(part.shape[0] * part.shape[1] for part in parts)


def part_shapes(rows, width, places):
    step = rows // sum(len(blocks) for blocks in places)
    return [(len(blocks), step, width) for blocks in places]


def add_swapped(own, got):
    rows = own.shape[0] // 2
    return own + jnp.concatenate([got[rows:], got[:rows]], axis=0).astype(F32)


def gate_up_kernel(places, *refs):
    count = len(places)
    parts, (gate, up, far_gate, far_up, rows, own, send) = refs[:count], refs[count:]

    @pl.when(pl.program_id(0) == 0)
    def _():
        gather_rows(parts, places, rows)

    block = gate.shape[1]
    near_x, far_x = rows[:, :block], rows[:, block:]
    for k, (near_w, far_w) in enumerate(((gate, far_gate), (up, far_up))):
        part = plain_dot(near_x, near_w[0]) + plain_dot(far_x, far_w[0])
        own[k] = part
        send[k] = part.astype(BF16)


def gate_up_parts(parts, places, w_gate, w_up, far_gate, far_up, tile):
    rows, half = row_count(parts), parts[0].shape[-1]
    _, block, hidden = w_gate.shape
    near = pl.BlockSpec((1, block, tile), lambda j: (0, 0, j))
    part = pl.BlockSpec((2, rows, tile), lambda j: (0, 0, j))
    return pl.pallas_call(
        functools.partial(gate_up_kernel, places),
        grid=(hidden // tile,),
        in_specs=[whole(part.shape) for part in parts]
        + [
            near,
            near,
            near,
            near,
        ],
        out_specs=[whole((rows, half)), part, part],
        out_shape=[
            jax.ShapeDtypeStruct((rows, half), BF16),
            jax.ShapeDtypeStruct((2, rows, hidden), F32),
            jax.ShapeDtypeStruct((2, rows, hidden), BF16),
        ],
        compiler_params=params(),
        cost_estimate=cost(0.01),
        name="gate_up_parts",
    )(*parts, w_gate, w_up, far_gate, far_up)


def grad_hidden_kernel(places, *refs):
    count = len(places)
    parts, (down, far_down, rows, own, send) = refs[:count], refs[count:]

    @pl.when(pl.program_id(0) == 0)
    def _():
        gather_rows(parts, places, rows)

    block = down.shape[2]
    part = contract_last(rows[:, :block], down[0]) + contract_last(rows[:, block:], far_down[0])
    own[...] = part
    send[...] = part.astype(BF16)


def grad_hidden_parts(parts, places, w_down, far_down, tile):
    rows, half = row_count(parts), parts[0].shape[-1]
    _, hidden, block = w_down.shape
    part = pl.BlockSpec((rows, tile), lambda j: (0, j))
    near = pl.BlockSpec((1, tile, block), lambda j: (0, j, 0))
    return pl.pallas_call(
        functools.partial(grad_hidden_kernel, places),
        grid=(hidden // tile,),
        in_specs=[whole(part.shape) for part in parts]
        + [
            near,
            near,
        ],
        out_specs=[whole((rows, half)), part, part],
        out_shape=[
            jax.ShapeDtypeStruct((rows, half), BF16),
            jax.ShapeDtypeStruct((rows, hidden), F32),
            jax.ShapeDtypeStruct((rows, hidden), BF16),
        ],
        compiler_params=params(),
        cost_estimate=cost(1),
        name="grad_hidden_parts",
    )(*parts, w_down, far_down)


def slot_out_kernel(places, own, got, down, far_down, grad_rows, hidden, far_grad, *refs):
    *out, total = refs
    step = pl.program_id(0)
    block = down.shape[2]
    gate_pre = add_swapped(own[0], got[0])
    up_pre = add_swapped(own[1], got[1])
    value = (gate_pre * jax.nn.sigmoid(gate_pre) * up_pre).astype(BF16)
    hidden[...] = value

    @pl.when(step == 0)
    def _():
        total[...] = jnp.zeros_like(total)

    total[:, :block] += plain_dot(value, down[0])
    total[:, block:] += plain_dot(value, far_down[0])
    far_grad[...] = contract_first(value, grad_rows[:, block:]).astype(BF16)

    @pl.when(step == pl.num_programs(0) - 1)
    def _():
        spread_rows(total[...], out, places)


def slot_out_parts(own, got, w_down, far_down, y, tile, places):
    _, rows, hidden = own.shape
    block = w_down.shape[2]
    part = pl.BlockSpec((2, rows, tile), lambda j: (0, 0, j))
    shapes = part_shapes(rows, 2 * block, places)
    near = pl.BlockSpec((1, tile, block), lambda j: (0, j, 0))
    return pl.pallas_call(
        functools.partial(slot_out_kernel, places),
        grid=(hidden // tile,),
        in_specs=[
            part,
            part,
            near,
            near,
            whole(y.shape),
        ],
        out_specs=[
            pl.BlockSpec((rows, tile), lambda j: (0, j)),
            pl.BlockSpec((tile, block), lambda j: (j, 0)),
        ]
        + [whole(shape) for shape in shapes],
        out_shape=[
            jax.ShapeDtypeStruct((rows, hidden), BF16),
            jax.ShapeDtypeStruct((hidden, block), BF16),
        ]
        + [jax.ShapeDtypeStruct(shape, BF16) for shape in shapes],
        scratch_shapes=[pltpu.VMEM((rows, 2 * block), F32)],
        compiler_params=params(),
        cost_estimate=cost(0.01),
        name="slot_out",
    )(own, got, w_down, far_down, y)


def slot_grad_kernel(
    places, own, got, own_grad, got_grad, gate, up, far_gate, far_up, rows,
    grads, far_grads, *refs,
):
    *out, total = refs
    step = pl.program_id(0)
    block = gate.shape[1]
    gate_pre = add_swapped(own[0], got[0])
    up_pre = add_swapped(own[1], got[1])
    grad_hidden = add_swapped(own_grad[...], got_grad[...])
    sigmoid_gate = jax.nn.sigmoid(gate_pre)
    grad_gate = (
        grad_hidden * up_pre * sigmoid_gate * (1.0 + gate_pre * (1.0 - sigmoid_gate))
    ).astype(BF16)
    grad_up = (grad_hidden * gate_pre * sigmoid_gate).astype(BF16)
    grads[0] = grad_gate
    grads[1] = grad_up
    far_grads[0] = contract_first(rows[:, block:], grad_gate).astype(BF16)
    far_grads[1] = contract_first(rows[:, block:], grad_up).astype(BF16)

    @pl.when(step == 0)
    def _():
        total[...] = jnp.zeros_like(total)

    total[:, :block] += contract_last(grad_gate, gate[0]) + contract_last(grad_up, up[0])
    total[:, block:] += contract_last(grad_gate, far_gate[0]) + contract_last(
        grad_up, far_up[0]
    )

    @pl.when(step == pl.num_programs(0) - 1)
    def _():
        spread_rows(total[...], out, places)


def slot_grad_parts(own, got, own_grad, got_grad, w_gate, w_up, far_gate, far_up, x, tile, places):
    _, rows, hidden = own.shape
    block = w_gate.shape[1]
    part = pl.BlockSpec((2, rows, tile), lambda j: (0, 0, j))
    near = pl.BlockSpec((1, block, tile), lambda j: (0, 0, j))
    grad_part = pl.BlockSpec((rows, tile), lambda j: (0, j))
    shapes = part_shapes(rows, 2 * block, places)
    return pl.pallas_call(
        functools.partial(slot_grad_kernel, places),
        grid=(hidden // tile,),
        in_specs=[
            part,
            part,
            grad_part,
            grad_part,
            near,
            near,
            near,
            near,
            whole(x.shape),
        ],
        out_specs=[
            part,
            pl.BlockSpec((2, block, tile), lambda j: (0, 0, j)),
        ]
        + [whole(shape) for shape in shapes],
        out_shape=[
            jax.ShapeDtypeStruct((2, rows, hidden), BF16),
            jax.ShapeDtypeStruct((2, block, hidden), BF16),
        ]
        + [jax.ShapeDtypeStruct(shape, BF16) for shape in shapes],
        scratch_shapes=[pltpu.VMEM((rows, 2 * block), F32)],
        compiler_params=params(),
        cost_estimate=cost(0),
        name="slot_grad",
    )(own, got, own_grad, got_grad, w_gate, w_up, far_gate, far_up, x)


def unslot_kernel(weighted, pick, weight, near, far, other, out):
    half_rows, half = near.shape
    block = half // 2
    replica, expert = lax.axis_index("dp"), lax.axis_index("expert")
    for j in range(4):
        start = pl.multiple_of((replica ^ offset(expert, j)) * block, block)
        own = (near if j < 2 else far)[:, pl.ds((j % 2) * block, block)]
        k = (0, 2, 1, 3)[j]
        rest = other[k // 2, :, pl.ds((k % 2) * block, block)]
        value = plain_dot(pick[:, :half_rows], own) + plain_dot(pick[:, half_rows:], rest)
        if weighted:
            value = weight[:, :1] * value
        out[:, pl.ds(start, block)] = value.astype(BF16)


def unslot(pick, weight, near, far, other, weighted):
    count = pick.shape[0]
    half_rows, half = near.shape
    return pl.pallas_call(
        functools.partial(unslot_kernel, weighted),
        out_shape=jax.ShapeDtypeStruct((count, 2 * half), BF16),
        compiler_params=params(),
        cost_estimate=cost(4),
        name="unslot",
    )(pick, weight, near, far, other)


def swap_chips(parts, chips, *earlier):
    got = list(parts)
    for first in range(0, len(parts), chips):
        for k in range(1, chips):
            got[first + k] = swap_expert(after(parts[first + k], *earlier), 2 * k)
    return got


def send_slots(slots, others, chips, capacity, apart, before_rows, before_near, before_far):
    half = slots.shape[-1]
    other = swap_expert(others, 1)
    far = swap_rows(after(jnp.stack([slots[1], other[1]], axis=0), *before_rows))

    def by_chip(own, rest):
        shape = (chips, 1, capacity, half)
        both = jnp.concatenate([own.reshape(shape), rest.reshape(shape)], axis=1)
        return [both[k].reshape(1, 2 * capacity, half) for k in range(chips)]

    near_parts, far_parts = by_chip(slots[0], other[0]), by_chip(far[0], far[1])
    if apart:
        near_parts = swap_chips(near_parts, chips, *before_near)
        for k in range(1, chips):
            far_parts[k] = after(far_parts[k], near_parts[k])
        return far, near_parts + swap_chips(far_parts, chips, *before_far)
    parts = [jnp.concatenate(pair, axis=0) for pair in zip(near_parts, far_parts)]
    return far, swap_chips(parts, chips, *before_near)


def return_slots(parts, chips, capacity, before_rows, before_core):
    half = parts[0].shape[-1]
    if len(parts) == chips:
        parts = [part[:1] for part in parts] + [part[1:] for part in parts]
    shape = (chips, 2, capacity, half)
    far = swap_rows(after(jnp.concatenate(parts[chips:], axis=0), *before_rows)).reshape(shape)
    near = jnp.concatenate(parts[:chips], axis=0).reshape(shape)
    rows = chips * capacity
    other = jnp.stack([near[:, 1].reshape(rows, half), far[:, 1].reshape(rows, half)], axis=0)
    other = swap_expert(after(other, *before_core), 1)
    return near[:, 0].reshape(rows, half), far[:, 0].reshape(rows, half), other


def body(tokens, cotangent, routes, gate_fixed, w_gate, w_up, w_down):
    tok_count, model_width = tokens.shape
    hidden_width = w_gate.shape[2]
    experts = lax.axis_size("expert")
    chips = experts // 2
    capacity = 3 * tok_count // (2 * experts)
    block = model_width // 4
    tile = 256 if hidden_width % 256 == 0 else hidden_width
    far_gate = swap_weight(w_gate)
    slots, others = make_slots(tokens, routes, gate_fixed, experts, capacity)
    grad_slots, grad_others, pick, weight = make_grads(
        cotangent, routes, gate_fixed, experts, capacity
    )
    far, got_parts = send_slots(
        slots, others, chips, capacity, True, (), (), ()
    )
    far_up = swap_weight(w_up)
    far_down = swap_weight(after(w_down, *(far,)))
    grad_far, got_grad_parts = send_slots(
        grad_slots, grad_others, chips, capacity, False, (far_up,), got_parts, got_parts
    )
    if (2 * capacity) % 16 == 0:
        apart = tuple((k,) for k in range(2 * chips))
        paired = tuple((k, k + chips) for k in range(chips))
    else:
        apart = paired = ((0,),)

    def joined(parts):
        if apart != paired:
            return parts
        if len(parts) == chips:
            parts = [part[:1] for part in parts] + [part[1:] for part in parts]
        return [jnp.concatenate(parts, axis=1)]

    def cut(parts):
        if apart != paired:
            return parts
        return jnp.split(parts[0], 2 * chips, axis=1)

    rows, own, send = gate_up_parts(
        joined(got_parts), apart, w_gate, w_up, far_gate, far_up, tile
    )
    got = swap_rows(send)
    grad_rows, own_grad, send_grad = grad_hidden_parts(
        joined(got_grad_parts), paired, after(w_down, *(send,)), far_down, tile
    )
    got_grad = swap_rows(send_grad)

    hidden, far_grad_down, *slot_out = slot_out_parts(
        own, got, w_down, far_down, grad_rows, tile, paired
    )
    out_parts = swap_chips(cut(slot_out), chips)
    sent = [part for k, part in enumerate(out_parts) if k % chips]
    got_down = swap_weight(far_grad_down)
    grads, far_grads, *slot_grad = slot_grad_parts(
        own,
        got,
        own_grad,
        after(got_grad, *(hidden,)),
        w_gate,
        w_up,
        far_gate,
        far_up,
        rows,
        tile,
        paired,
    )
    grad_out_parts = cut(slot_grad)
    for k in range(len(grad_out_parts)):
        if k % chips:
            value = after(grad_out_parts[k], out_parts[k % chips])
            grad_out_parts[k] = swap_expert(value, 2 * (k % chips))
    got_far = swap_weight(after(far_grads, *sent[:1]))

    grad_w_gate = contract_first(rows[:, :block], grads[0]) + got_far[0].astype(F32)
    grad_w_up = contract_first(rows[:, :block], grads[1]) + got_far[1].astype(F32)
    grad_w_down = contract_first(hidden, grad_rows[:, :block]) + got_down.astype(F32)
    grad_w_gate, grad_w_up, grad_w_down = (
        value.astype(BF16)[None] for value in (grad_w_gate, grad_w_up, grad_w_down)
    )

    back = return_slots(out_parts, chips, capacity, (slot_grad[0],), ())
    mixed = unslot(pick, weight, *back, True)
    grad_back = return_slots(grad_out_parts, chips, capacity, (), (mixed,))
    grad_tokens = unslot(pick, weight, *grad_back, False)
    return (
        mixed,
        grad_tokens,
        grad_w_gate,
        grad_w_up,
        grad_w_down,
    )


def solution(mesh):
    return jax.shard_map(
        body,
        mesh=mesh,
        in_specs=(
            P(("dp", "expert"), None),
            P(("dp", "expert"), None),
            P(("dp", "expert"), None),
            P(("dp", "expert"), None),
            P("expert", "dp", None),
            P("expert", "dp", None),
            P("expert", None, "dp"),
        ),
        out_specs=(
            P(("dp", "expert"), None),
            P(("dp", "expert"), None),
            P("expert", "dp", None),
            P("expert", "dp", None),
            P("expert", None, "dp"),
        ),
        check_vma=False,
    )
```

```python
import functools

import jax
import jax.numpy as jnp
from jax import lax
from jax.experimental import pallas as pl
from jax.experimental.pallas import tpu as pltpu
from jax.sharding import PartitionSpec as P

BOTH = ("dp", "expert")
VMEM_BYTES = 40 * 2**20
F32 = jnp.float32
BF16 = jnp.bfloat16


def contract_last(left_side, right_side):
    return lax.dot_general(
        left_side, right_side, (((1,), (1,)), ((), ())), preferred_element_type=F32
    )


def contract_first(left_side, right_side):
    return lax.dot_general(
        left_side, right_side, (((0,), (0,)), ((), ())), preferred_element_type=F32
    )


def plain_dot(left_side, right_side):
    return jnp.dot(left_side, right_side, preferred_element_type=F32)


def pair_list(experts, masks):
    return [
        (replica * experts + expert, (replica ^ masks[expert % 2]) * experts + expert)
        for replica in range(4)
        for expert in range(experts)
    ]


def swap_weight(value):
    return lax.ppermute(value, BOTH, pair_list(lax.axis_size("expert"), (1, 2)))


def swap_rows(value):
    return lax.ppermute(value, BOTH, pair_list(lax.axis_size("expert"), (2, 1)))


def swap_expert(value, mask):
    experts = lax.axis_size("expert")
    return lax.ppermute(value, "expert", [(i, i ^ mask) for i in range(experts)])


def offset(expert, j):
    side = 1 + (expert & 1)
    return (0, side, 3 - side, 3)[j]


def after(value, *earlier):
    return lax.optimization_barrier((value,) + earlier)[0]


def params(limit=VMEM_BYTES):
    return pltpu.CompilerParams(vmem_limit_bytes=limit)


def cost(microseconds):
    return pl.CostEstimate(
        flops=int(microseconds * 1e9), bytes_accessed=int(microseconds * 3e6), transcendentals=0
    )


def whole(shape):
    return pl.BlockSpec(shape, lambda *_: (0,) * len(shape))


def choose(experts, capacity, route, fixed):
    chips = experts // 2
    tokens = route.shape[1]
    routes = route[...]
    expert = lax.axis_index("expert")
    expert_row = lax.broadcasted_iota(jnp.int32, (experts, tokens), 0)
    one_hot = jnp.where(expert_row == routes, 1.0, 0.0)
    earlier = jnp.where(
        lax.broadcasted_iota(jnp.int32, (tokens, tokens), 0)
        < lax.broadcasted_iota(jnp.int32, (tokens, tokens), 1),
        1.0,
        0.0,
    )
    before = plain_dot(one_hot.astype(BF16), earlier.astype(BF16))
    position = jnp.sum(before * one_hot, axis=0, keepdims=True).astype(jnp.int32)
    relative = routes ^ expert
    slot = ((relative & 1) * chips + (relative >> 1)) * capacity + position
    rows = experts * capacity
    chosen = jnp.where(lax.broadcasted_iota(jnp.int32, (rows, tokens), 0) == slot, 1.0, 0.0)
    return chosen, fixed[...].astype(F32) / 65536.0


def fill(chosen, scale, source, *outs):
    half_rows = chosen.shape[0] // 2
    block = source.shape[1] // 4
    replica, expert = lax.axis_index("dp"), lax.axis_index("expert")
    chosen = chosen.astype(BF16)
    for core, out in enumerate(outs):
        part = chosen[core * half_rows : (core + 1) * half_rows]
        for j in range(4):
            start = pl.multiple_of((replica ^ offset(expert + core, j)) * block, block)
            value = plain_dot(part, source[:, pl.ds(start, block)])
            if scale is not None:
                value = scale[core * half_rows : (core + 1) * half_rows] * value
            out[j // 2, :, pl.ds((j % 2) * block, block)] = value.astype(BF16)


def slot_kernel(experts, capacity, tok, route, fixed, own, other):
    chosen, _ = choose(experts, capacity, route, fixed)
    fill(chosen, None, tok, own, other)


def grad_kernel(experts, capacity, cot, route, fixed, own, other, pick, weight):
    chosen, route_weight = choose(experts, capacity, route, fixed)
    tokens = cot.shape[0]
    pick[...] = jnp.transpose(chosen).astype(BF16)
    weight[...] = jnp.transpose(jnp.broadcast_to(route_weight, (tokens, tokens)))
    fill(chosen, jnp.sum(chosen * route_weight, axis=1, keepdims=True), cot, own, other)


def make_slots(tokens, routes, gate_fixed, experts, capacity):
    count, width = tokens.shape
    slot_shape = jax.ShapeDtypeStruct((2, experts * capacity // 2, width // 2), BF16)
    return pl.pallas_call(
        functools.partial(slot_kernel, experts, capacity),
        out_shape=[slot_shape] * 2,
        compiler_params=params(60 * 2**20),
        cost_estimate=cost(0.01),
        name="make_slots",
    )(tokens, routes.reshape(1, count), gate_fixed.reshape(1, count))


def make_grads(cotangent, routes, gate_fixed, experts, capacity):
    count, width = cotangent.shape
    slot_shape = jax.ShapeDtypeStruct((2, experts * capacity // 2, width // 2), BF16)
    return pl.pallas_call(
        functools.partial(grad_kernel, experts, capacity),
        out_shape=[slot_shape] * 2
        + [
            jax.ShapeDtypeStruct((count, experts * capacity), BF16),
            jax.ShapeDtypeStruct((count, count), F32),
        ],
        compiler_params=params(60 * 2**20),
        cost_estimate=cost(0.01),
        name="make_grads",
    )(cotangent, routes.reshape(1, count), gate_fixed.reshape(1, count))


def gather_rows(parts, places, out):
    for part, blocks in zip(parts, places):
        step = part.shape[1]
        for i, block in enumerate(blocks):
            out[pl.ds(block * step, step), :] = part[i]


def spread_rows(value, parts, places):
    for part, blocks in zip(parts, places):
        step = part.shape[1]
        for i, block in enumerate(blocks):
            part[i] = value[block * step : (block + 1) * step].astype(BF16)


def row_count(parts):
    return sum(part.shape[0] * part.shape[1] for part in parts)


def part_shapes(rows, width, places):
    step = rows // sum(len(blocks) for blocks in places)
    return [(len(blocks), step, width) for blocks in places]


def add_swapped(own, got):
    rows = own.shape[0] // 2
    return own + jnp.concatenate([got[rows:], got[:rows]], axis=0).astype(F32)


def gate_up_kernel(places, *refs):
    count = len(places)
    parts, (gate, up, far_gate, far_up, rows, own, send) = refs[:count], refs[count:]

    @pl.when(pl.program_id(0) == 0)
    def _():
        gather_rows(parts, places, rows)

    block = gate.shape[1]
    near_x, far_x = rows[:, :block], rows[:, block:]
    for k, (near_w, far_w) in enumerate(((gate, far_gate), (up, far_up))):
        part = plain_dot(near_x, near_w[0]) + plain_dot(far_x, far_w[0])
        own[k] = part
        send[k] = part.astype(BF16)


def gate_up_parts(parts, places, w_gate, w_up, far_gate, far_up, tile):
    rows, half = row_count(parts), parts[0].shape[-1]
    _, block, hidden = w_gate.shape
    near = pl.BlockSpec((1, block, tile), lambda j: (0, 0, j))
    part = pl.BlockSpec((2, rows, tile), lambda j: (0, 0, j))
    return pl.pallas_call(
        functools.partial(gate_up_kernel, places),
        grid=(hidden // tile,),
        in_specs=[whole(part.shape) for part in parts]
        + [
            near,
            near,
            near,
            near,
        ],
        out_specs=[whole((rows, half)), part, part],
        out_shape=[
            jax.ShapeDtypeStruct((rows, half), BF16),
            jax.ShapeDtypeStruct((2, rows, hidden), F32),
            jax.ShapeDtypeStruct((2, rows, hidden), BF16),
        ],
        compiler_params=params(),
        cost_estimate=cost(0.01),
        name="gate_up_parts",
    )(*parts, w_gate, w_up, far_gate, far_up)


def grad_hidden_kernel(places, *refs):
    count = len(places)
    parts, (down, far_down, rows, own, send) = refs[:count], refs[count:]

    @pl.when(pl.program_id(0) == 0)
    def _():
        gather_rows(parts, places, rows)

    block = down.shape[2]
    part = contract_last(rows[:, :block], down[0]) + contract_last(rows[:, block:], far_down[0])
    own[...] = part
    send[...] = part.astype(BF16)


def grad_hidden_parts(parts, places, w_down, far_down, tile):
    rows, half = row_count(parts), parts[0].shape[-1]
    _, hidden, block = w_down.shape
    part = pl.BlockSpec((rows, tile), lambda j: (0, j))
    near = pl.BlockSpec((1, tile, block), lambda j: (0, j, 0))
    return pl.pallas_call(
        functools.partial(grad_hidden_kernel, places),
        grid=(hidden // tile,),
        in_specs=[whole(part.shape) for part in parts]
        + [
            near,
            near,
        ],
        out_specs=[whole((rows, half)), part, part],
        out_shape=[
            jax.ShapeDtypeStruct((rows, half), BF16),
            jax.ShapeDtypeStruct((rows, hidden), F32),
            jax.ShapeDtypeStruct((rows, hidden), BF16),
        ],
        compiler_params=params(),
        cost_estimate=cost(1),
        name="grad_hidden_parts",
    )(*parts, w_down, far_down)


def slot_out_kernel(places, own, got, down, far_down, grad_rows, hidden, far_grad, *refs):
    *out, total = refs
    step = pl.program_id(0)
    block = down.shape[2]
    gate_pre = add_swapped(own[0], got[0])
    up_pre = add_swapped(own[1], got[1])
    value = (gate_pre * jax.nn.sigmoid(gate_pre) * up_pre).astype(BF16)
    hidden[...] = value

    @pl.when(step == 0)
    def _():
        total[...] = jnp.zeros_like(total)

    total[:, :block] += plain_dot(value, down[0])
    total[:, block:] += plain_dot(value, far_down[0])
    far_grad[...] = contract_first(value, grad_rows[:, block:]).astype(BF16)

    @pl.when(step == pl.num_programs(0) - 1)
    def _():
        spread_rows(total[...], out, places)


def slot_out_parts(own, got, w_down, far_down, y, tile, places):
    _, rows, hidden = own.shape
    block = w_down.shape[2]
    part = pl.BlockSpec((2, rows, tile), lambda j: (0, 0, j))
    shapes = part_shapes(rows, 2 * block, places)
    near = pl.BlockSpec((1, tile, block), lambda j: (0, j, 0))
    return pl.pallas_call(
        functools.partial(slot_out_kernel, places),
        grid=(hidden // tile,),
        in_specs=[
            part,
            part,
            near,
            near,
            whole(y.shape),
        ],
        out_specs=[
            pl.BlockSpec((rows, tile), lambda j: (0, j)),
            pl.BlockSpec((tile, block), lambda j: (j, 0)),
        ]
        + [whole(shape) for shape in shapes],
        out_shape=[
            jax.ShapeDtypeStruct((rows, hidden), BF16),
            jax.ShapeDtypeStruct((hidden, block), BF16),
        ]
        + [jax.ShapeDtypeStruct(shape, BF16) for shape in shapes],
        scratch_shapes=[pltpu.VMEM((rows, 2 * block), F32)],
        compiler_params=params(),
        cost_estimate=cost(0.01),
        name="slot_out",
    )(own, got, w_down, far_down, y)


def slot_grad_kernel(
    places, own, got, own_grad, got_grad, gate, up, far_gate, far_up, rows,
    grads, far_grads, *refs,
):
    *out, total = refs
    step = pl.program_id(0)
    block = gate.shape[1]
    gate_pre = add_swapped(own[0], got[0])
    up_pre = add_swapped(own[1], got[1])
    grad_hidden = add_swapped(own_grad[...], got_grad[...])
    sigmoid_gate = jax.nn.sigmoid(gate_pre)
    grad_gate = (
        grad_hidden * up_pre * sigmoid_gate * (1.0 + gate_pre * (1.0 - sigmoid_gate))
    ).astype(BF16)
    grad_up = (grad_hidden * gate_pre * sigmoid_gate).astype(BF16)
    grads[0] = grad_gate
    grads[1] = grad_up
    far_grads[0] = contract_first(rows[:, block:], grad_gate).astype(BF16)
    far_grads[1] = contract_first(rows[:, block:], grad_up).astype(BF16)

    @pl.when(step == 0)
    def _():
        total[...] = jnp.zeros_like(total)

    total[:, :block] += contract_last(grad_gate, gate[0]) + contract_last(grad_up, up[0])
    total[:, block:] += contract_last(grad_gate, far_gate[0]) + contract_last(
        grad_up, far_up[0]
    )

    @pl.when(step == pl.num_programs(0) - 1)
    def _():
        spread_rows(total[...], out, places)


def slot_grad_parts(own, got, own_grad, got_grad, w_gate, w_up, far_gate, far_up, x, tile, places):
    _, rows, hidden = own.shape
    block = w_gate.shape[1]
    part = pl.BlockSpec((2, rows, tile), lambda j: (0, 0, j))
    near = pl.BlockSpec((1, block, tile), lambda j: (0, 0, j))
    grad_part = pl.BlockSpec((rows, tile), lambda j: (0, j))
    shapes = part_shapes(rows, 2 * block, places)
    return pl.pallas_call(
        functools.partial(slot_grad_kernel, places),
        grid=(hidden // tile,),
        in_specs=[
            part,
            part,
            grad_part,
            grad_part,
            near,
            near,
            near,
            near,
            whole(x.shape),
        ],
        out_specs=[
            part,
            pl.BlockSpec((2, block, tile), lambda j: (0, 0, j)),
        ]
        + [whole(shape) for shape in shapes],
        out_shape=[
            jax.ShapeDtypeStruct((2, rows, hidden), BF16),
            jax.ShapeDtypeStruct((2, block, hidden), BF16),
        ]
        + [jax.ShapeDtypeStruct(shape, BF16) for shape in shapes],
        scratch_shapes=[pltpu.VMEM((rows, 2 * block), F32)],
        compiler_params=params(),
        cost_estimate=cost(0),
        name="slot_grad",
    )(own, got, own_grad, got_grad, w_gate, w_up, far_gate, far_up, x)


def unslot_kernel(weighted, pick, weight, near, far, other, out):
    half_rows, half = near.shape
    block = half // 2
    replica, expert = lax.axis_index("dp"), lax.axis_index("expert")
    for j in range(4):
        start = pl.multiple_of((replica ^ offset(expert, j)) * block, block)
        own = (near if j < 2 else far)[:, pl.ds((j % 2) * block, block)]
        k = (0, 2, 1, 3)[j]
        rest = other[k // 2, :, pl.ds((k % 2) * block, block)]
        value = plain_dot(pick[:, :half_rows], own) + plain_dot(pick[:, half_rows:], rest)
        if weighted:
            value = weight[:, :1] * value
        out[:, pl.ds(start, block)] = value.astype(BF16)


def unslot(pick, weight, near, far, other, weighted):
    count = pick.shape[0]
    half_rows, half = near.shape
    return pl.pallas_call(
        functools.partial(unslot_kernel, weighted),
        out_shape=jax.ShapeDtypeStruct((count, 2 * half), BF16),
        compiler_params=params(),
        cost_estimate=cost(4),
        name="unslot",
    )(pick, weight, near, far, other)


def swap_chips(parts, chips, *earlier):
    got = list(parts)
    for first in range(0, len(parts), chips):
        for k in range(1, chips):
            got[first + k] = swap_expert(after(parts[first + k], *earlier), 2 * k)
    return got


def send_slots(slots, others, chips, capacity, apart, before_rows, before_near, before_far):
    half = slots.shape[-1]
    other = swap_expert(others, 1)
    far = swap_rows(after(jnp.stack([slots[1], other[1]], axis=0), *before_rows))

    def by_chip(own, rest):
        shape = (chips, 1, capacity, half)
        both = jnp.concatenate([own.reshape(shape), rest.reshape(shape)], axis=1)
        return [both[k].reshape(1, 2 * capacity, half) for k in range(chips)]

    near_parts, far_parts = by_chip(slots[0], other[0]), by_chip(far[0], far[1])
    if apart:
        near_parts = swap_chips(near_parts, chips, *before_near)
        for k in range(1, chips):
            far_parts[k] = after(far_parts[k], near_parts[k])
        return far, near_parts + swap_chips(far_parts, chips, *before_far)
    parts = [jnp.concatenate(pair, axis=0) for pair in zip(near_parts, far_parts)]
    return far, swap_chips(parts, chips, *before_near)


def return_slots(parts, chips, capacity, before_rows, before_core):
    half = parts[0].shape[-1]
    if len(parts) == chips:
        parts = [part[:1] for part in parts] + [part[1:] for part in parts]
    shape = (chips, 2, capacity, half)
    far = swap_rows(after(jnp.concatenate(parts[chips:], axis=0), *before_rows)).reshape(shape)
    near = jnp.concatenate(parts[:chips], axis=0).reshape(shape)
    rows = chips * capacity
    other = jnp.stack([near[:, 1].reshape(rows, half), far[:, 1].reshape(rows, half)], axis=0)
    other = swap_expert(after(other, *before_core), 1)
    return near[:, 0].reshape(rows, half), far[:, 0].reshape(rows, half), other


def body(tokens, cotangent, routes, gate_fixed, w_gate, w_up, w_down):
    tok_count, model_width = tokens.shape
    hidden_width = w_gate.shape[2]
    experts = lax.axis_size("expert")
    chips = experts // 2
    capacity = 3 * tok_count // (2 * experts)
    block = model_width // 4
    tile = 256 if hidden_width % 256 == 0 else hidden_width
    far_gate = swap_weight(w_gate)
    slots, others = make_slots(tokens, routes, gate_fixed, experts, capacity)
    grad_slots, grad_others, pick, weight = make_grads(
        cotangent, routes, gate_fixed, experts, capacity
    )
    far, got_parts = send_slots(
        slots, others, chips, capacity, True, (), (), ()
    )
    far_up = swap_weight(w_up)
    far_down = swap_weight(after(w_down, *(far,)))
    grad_far, got_grad_parts = send_slots(
        grad_slots, grad_others, chips, capacity, False, (far_up,), got_parts, got_parts
    )
    if (2 * capacity) % 16 == 0:
        apart = tuple((k,) for k in range(2 * chips))
        paired = tuple((k, k + chips) for k in range(chips))
    else:
        apart = paired = ((0,),)

    def joined(parts):
        if apart != paired:
            return parts
        if len(parts) == chips:
            parts = [part[:1] for part in parts] + [part[1:] for part in parts]
        return [jnp.concatenate(parts, axis=1)]

    def cut(parts):
        if apart != paired:
            return parts
        return jnp.split(parts[0], 2 * chips, axis=1)

    rows, own, send = gate_up_parts(
        joined(got_parts), apart, w_gate, w_up, far_gate, far_up, tile
    )
    got = swap_rows(send)
    grad_rows, own_grad, send_grad = grad_hidden_parts(
        joined(got_grad_parts), paired, after(w_down, *(send,)), far_down, tile
    )
    got_grad = swap_rows(send_grad)

    hidden, far_grad_down, *slot_out = slot_out_parts(
        own, got, w_down, far_down, grad_rows, tile, paired
    )
    out_parts = swap_chips(cut(slot_out), chips)
    sent = [part for k, part in enumerate(out_parts) if k % chips]
    got_down = swap_weight(after(far_grad_down, *(got_grad,)))
    grads, far_grads, *slot_grad = slot_grad_parts(
        own,
        got,
        own_grad,
        after(got_grad, *(hidden,)),
        w_gate,
        w_up,
        far_gate,
        far_up,
        rows,
        tile,
        paired,
    )
    grad_out_parts = cut(slot_grad)
    for k in range(len(grad_out_parts)):
        if k % chips:
            value = after(grad_out_parts[k], out_parts[k % chips])
            grad_out_parts[k] = swap_expert(value, 2 * (k % chips))
    got_far = swap_weight(after(far_grads, *sent[1:2]))

    grad_w_gate = contract_first(rows[:, :block], grads[0]) + got_far[0].astype(F32)
    grad_w_up = contract_first(rows[:, :block], grads[1]) + got_far[1].astype(F32)
    grad_w_down = contract_first(hidden, grad_rows[:, :block]) + got_down.astype(F32)
    grad_w_gate, grad_w_up, grad_w_down = (
        value.astype(BF16)[None] for value in (grad_w_gate, grad_w_up, grad_w_down)
    )

    back = return_slots(out_parts, chips, capacity, (slot_grad[0],), ())
    mixed = unslot(pick, weight, *back, True)
    grad_back = return_slots(grad_out_parts, chips, capacity, (), (mixed,))
    grad_tokens = unslot(pick, weight, *grad_back, False)
    return (
        mixed,
        grad_tokens,
        grad_w_gate,
        grad_w_up,
        grad_w_down,
    )


def solution(mesh):
    return jax.shard_map(
        body,
        mesh=mesh,
        in_specs=(
            P(("dp", "expert"), None),
            P(("dp", "expert"), None),
            P(("dp", "expert"), None),
            P(("dp", "expert"), None),
            P("expert", "dp", None),
            P("expert", "dp", None),
            P("expert", None, "dp"),
        ),
        out_specs=(
            P(("dp", "expert"), None),
            P(("dp", "expert"), None),
            P("expert", "dp", None),
            P("expert", "dp", None),
            P("expert", None, "dp"),
        ),
        check_vma=False,
    )
```

```python
import functools

import jax
import jax.numpy as jnp
from jax import lax
from jax.experimental import pallas as pl
from jax.experimental.pallas import tpu as pltpu
from jax.sharding import PartitionSpec as P

BOTH = ("dp", "expert")
VMEM_BYTES = 40 * 2**20
F32 = jnp.float32
BF16 = jnp.bfloat16


def contract_last(left_side, right_side):
    return lax.dot_general(
        left_side, right_side, (((1,), (1,)), ((), ())), preferred_element_type=F32
    )


def contract_first(left_side, right_side):
    return lax.dot_general(
        left_side, right_side, (((0,), (0,)), ((), ())), preferred_element_type=F32
    )


def plain_dot(left_side, right_side):
    return jnp.dot(left_side, right_side, preferred_element_type=F32)


def pair_list(experts, masks):
    return [
        (replica * experts + expert, (replica ^ masks[expert % 2]) * experts + expert)
        for replica in range(4)
        for expert in range(experts)
    ]


def swap_weight(value):
    return lax.ppermute(value, BOTH, pair_list(lax.axis_size("expert"), (1, 2)))


def swap_rows(value):
    return lax.ppermute(value, BOTH, pair_list(lax.axis_size("expert"), (2, 1)))


def swap_expert(value, mask):
    experts = lax.axis_size("expert")
    return lax.ppermute(value, "expert", [(i, i ^ mask) for i in range(experts)])


def offset(expert, j):
    side = 1 + (expert & 1)
    return (0, side, 3 - side, 3)[j]


def after(value, *earlier):
    return lax.optimization_barrier((value,) + earlier)[0]


def params(limit=VMEM_BYTES):
    return pltpu.CompilerParams(vmem_limit_bytes=limit)


def cost(microseconds):
    return pl.CostEstimate(
        flops=int(microseconds * 1e9), bytes_accessed=int(microseconds * 3e6), transcendentals=0
    )


def whole(shape):
    return pl.BlockSpec(shape, lambda *_: (0,) * len(shape))


def choose(experts, capacity, route, fixed):
    chips = experts // 2
    tokens = route.shape[1]
    routes = route[...]
    expert = lax.axis_index("expert")
    expert_row = lax.broadcasted_iota(jnp.int32, (experts, tokens), 0)
    one_hot = jnp.where(expert_row == routes, 1.0, 0.0)
    earlier = jnp.where(
        lax.broadcasted_iota(jnp.int32, (tokens, tokens), 0)
        < lax.broadcasted_iota(jnp.int32, (tokens, tokens), 1),
        1.0,
        0.0,
    )
    before = plain_dot(one_hot.astype(BF16), earlier.astype(BF16))
    position = jnp.sum(before * one_hot, axis=0, keepdims=True).astype(jnp.int32)
    relative = routes ^ expert
    slot = ((relative & 1) * chips + (relative >> 1)) * capacity + position
    rows = experts * capacity
    chosen = jnp.where(lax.broadcasted_iota(jnp.int32, (rows, tokens), 0) == slot, 1.0, 0.0)
    return chosen, fixed[...].astype(F32) / 65536.0


def fill(chosen, scale, source, *outs):
    half_rows = chosen.shape[0] // 2
    block = source.shape[1] // 4
    replica, expert = lax.axis_index("dp"), lax.axis_index("expert")
    chosen = chosen.astype(BF16)
    for core, out in enumerate(outs):
        part = chosen[core * half_rows : (core + 1) * half_rows]
        for j in range(4):
            start = pl.multiple_of((replica ^ offset(expert + core, j)) * block, block)
            value = plain_dot(part, source[:, pl.ds(start, block)])
            if scale is not None:
                value = scale[core * half_rows : (core + 1) * half_rows] * value
            out[j // 2, :, pl.ds((j % 2) * block, block)] = value.astype(BF16)


def slot_kernel(experts, capacity, tok, route, fixed, own, other):
    chosen, _ = choose(experts, capacity, route, fixed)
    fill(chosen, None, tok, own, other)


def grad_kernel(experts, capacity, cot, route, fixed, own, other, pick, weight):
    chosen, route_weight = choose(experts, capacity, route, fixed)
    tokens = cot.shape[0]
    pick[...] = jnp.transpose(chosen).astype(BF16)
    weight[...] = jnp.transpose(jnp.broadcast_to(route_weight, (tokens, tokens)))
    fill(chosen, jnp.sum(chosen * route_weight, axis=1, keepdims=True), cot, own, other)


def make_slots(tokens, routes, gate_fixed, experts, capacity):
    count, width = tokens.shape
    slot_shape = jax.ShapeDtypeStruct((2, experts * capacity // 2, width // 2), BF16)
    return pl.pallas_call(
        functools.partial(slot_kernel, experts, capacity),
        out_shape=[slot_shape] * 2,
        compiler_params=params(60 * 2**20),
        cost_estimate=cost(0.01),
        name="make_slots",
    )(tokens, routes.reshape(1, count), gate_fixed.reshape(1, count))


def make_grads(cotangent, routes, gate_fixed, experts, capacity):
    count, width = cotangent.shape
    slot_shape = jax.ShapeDtypeStruct((2, experts * capacity // 2, width // 2), BF16)
    return pl.pallas_call(
        functools.partial(grad_kernel, experts, capacity),
        out_shape=[slot_shape] * 2
        + [
            jax.ShapeDtypeStruct((count, experts * capacity), BF16),
            jax.ShapeDtypeStruct((count, count), F32),
        ],
        compiler_params=params(60 * 2**20),
        cost_estimate=cost(0.01),
        name="make_grads",
    )(cotangent, routes.reshape(1, count), gate_fixed.reshape(1, count))


def gather_rows(parts, places, out):
    for part, blocks in zip(parts, places):
        step = part.shape[1]
        for i, block in enumerate(blocks):
            out[pl.ds(block * step, step), :] = part[i]


def spread_rows(value, parts, places):
    for part, blocks in zip(parts, places):
        step = part.shape[1]
        for i, block in enumerate(blocks):
            part[i] = value[block * step : (block + 1) * step].astype(BF16)


def row_count(parts):
    return sum(part.shape[0] * part.shape[1] for part in parts)


def part_shapes(rows, width, places):
    step = rows // sum(len(blocks) for blocks in places)
    return [(len(blocks), step, width) for blocks in places]


def add_swapped(own, got):
    rows = own.shape[0] // 2
    return own + jnp.concatenate([got[rows:], got[:rows]], axis=0).astype(F32)


def gate_up_kernel(places, *refs):
    count = len(places)
    parts, (gate, up, far_gate, far_up, rows, own, send) = refs[:count], refs[count:]

    @pl.when(pl.program_id(0) == 0)
    def _():
        gather_rows(parts, places, rows)

    block = gate.shape[1]
    near_x, far_x = rows[:, :block], rows[:, block:]
    for k, (near_w, far_w) in enumerate(((gate, far_gate), (up, far_up))):
        part = plain_dot(near_x, near_w[0]) + plain_dot(far_x, far_w[0])
        own[k] = part
        send[k] = part.astype(BF16)


def gate_up_parts(parts, places, w_gate, w_up, far_gate, far_up, tile):
    rows, half = row_count(parts), parts[0].shape[-1]
    _, block, hidden = w_gate.shape
    near = pl.BlockSpec((1, block, tile), lambda j: (0, 0, j))
    part = pl.BlockSpec((2, rows, tile), lambda j: (0, 0, j))
    return pl.pallas_call(
        functools.partial(gate_up_kernel, places),
        grid=(hidden // tile,),
        in_specs=[whole(part.shape) for part in parts]
        + [
            near,
            near,
            near,
            near,
        ],
        out_specs=[whole((rows, half)), part, part],
        out_shape=[
            jax.ShapeDtypeStruct((rows, half), BF16),
            jax.ShapeDtypeStruct((2, rows, hidden), F32),
            jax.ShapeDtypeStruct((2, rows, hidden), BF16),
        ],
        compiler_params=params(),
        cost_estimate=cost(0.01),
        name="gate_up_parts",
    )(*parts, w_gate, w_up, far_gate, far_up)


def grad_hidden_kernel(places, *refs):
    count = len(places)
    parts, (down, far_down, rows, own, send) = refs[:count], refs[count:]

    @pl.when(pl.program_id(0) == 0)
    def _():
        gather_rows(parts, places, rows)

    block = down.shape[2]
    part = contract_last(rows[:, :block], down[0]) + contract_last(rows[:, block:], far_down[0])
    own[...] = part
    send[...] = part.astype(BF16)


def grad_hidden_parts(parts, places, w_down, far_down, tile):
    rows, half = row_count(parts), parts[0].shape[-1]
    _, hidden, block = w_down.shape
    part = pl.BlockSpec((rows, tile), lambda j: (0, j))
    near = pl.BlockSpec((1, tile, block), lambda j: (0, j, 0))
    return pl.pallas_call(
        functools.partial(grad_hidden_kernel, places),
        grid=(hidden // tile,),
        in_specs=[whole(part.shape) for part in parts]
        + [
            near,
            near,
        ],
        out_specs=[whole((rows, half)), part, part],
        out_shape=[
            jax.ShapeDtypeStruct((rows, half), BF16),
            jax.ShapeDtypeStruct((rows, hidden), F32),
            jax.ShapeDtypeStruct((rows, hidden), BF16),
        ],
        compiler_params=params(),
        cost_estimate=cost(1),
        name="grad_hidden_parts",
    )(*parts, w_down, far_down)


def slot_out_kernel(places, own, got, down, far_down, grad_rows, hidden, far_grad, *refs):
    *out, total = refs
    step = pl.program_id(0)
    block = down.shape[2]
    gate_pre = add_swapped(own[0], got[0])
    up_pre = add_swapped(own[1], got[1])
    value = (gate_pre * jax.nn.sigmoid(gate_pre) * up_pre).astype(BF16)
    hidden[...] = value

    @pl.when(step == 0)
    def _():
        total[...] = jnp.zeros_like(total)

    total[:, :block] += plain_dot(value, down[0])
    total[:, block:] += plain_dot(value, far_down[0])
    far_grad[...] = contract_first(value, grad_rows[:, block:]).astype(BF16)

    @pl.when(step == pl.num_programs(0) - 1)
    def _():
        spread_rows(total[...], out, places)


def slot_out_parts(own, got, w_down, far_down, y, tile, places):
    _, rows, hidden = own.shape
    block = w_down.shape[2]
    part = pl.BlockSpec((2, rows, tile), lambda j: (0, 0, j))
    shapes = part_shapes(rows, 2 * block, places)
    near = pl.BlockSpec((1, tile, block), lambda j: (0, j, 0))
    return pl.pallas_call(
        functools.partial(slot_out_kernel, places),
        grid=(hidden // tile,),
        in_specs=[
            part,
            part,
            near,
            near,
            whole(y.shape),
        ],
        out_specs=[
            pl.BlockSpec((rows, tile), lambda j: (0, j)),
            pl.BlockSpec((tile, block), lambda j: (j, 0)),
        ]
        + [whole(shape) for shape in shapes],
        out_shape=[
            jax.ShapeDtypeStruct((rows, hidden), BF16),
            jax.ShapeDtypeStruct((hidden, block), BF16),
        ]
        + [jax.ShapeDtypeStruct(shape, BF16) for shape in shapes],
        scratch_shapes=[pltpu.VMEM((rows, 2 * block), F32)],
        compiler_params=params(),
        cost_estimate=cost(0.01),
        name="slot_out",
    )(own, got, w_down, far_down, y)


def slot_grad_kernel(
    places, own, got, own_grad, got_grad, gate, up, far_gate, far_up, rows,
    grads, far_grads, *refs,
):
    *out, total = refs
    step = pl.program_id(0)
    block = gate.shape[1]
    gate_pre = add_swapped(own[0], got[0])
    up_pre = add_swapped(own[1], got[1])
    grad_hidden = add_swapped(own_grad[...], got_grad[...])
    sigmoid_gate = jax.nn.sigmoid(gate_pre)
    grad_gate = (
        grad_hidden * up_pre * sigmoid_gate * (1.0 + gate_pre * (1.0 - sigmoid_gate))
    ).astype(BF16)
    grad_up = (grad_hidden * gate_pre * sigmoid_gate).astype(BF16)
    grads[0] = grad_gate
    grads[1] = grad_up
    far_grads[0] = contract_first(rows[:, block:], grad_gate).astype(BF16)
    far_grads[1] = contract_first(rows[:, block:], grad_up).astype(BF16)

    @pl.when(step == 0)
    def _():
        total[...] = jnp.zeros_like(total)

    total[:, :block] += contract_last(grad_gate, gate[0]) + contract_last(grad_up, up[0])
    total[:, block:] += contract_last(grad_gate, far_gate[0]) + contract_last(
        grad_up, far_up[0]
    )

    @pl.when(step == pl.num_programs(0) - 1)
    def _():
        spread_rows(total[...], out, places)


def slot_grad_parts(own, got, own_grad, got_grad, w_gate, w_up, far_gate, far_up, x, tile, places):
    _, rows, hidden = own.shape
    block = w_gate.shape[1]
    part = pl.BlockSpec((2, rows, tile), lambda j: (0, 0, j))
    near = pl.BlockSpec((1, block, tile), lambda j: (0, 0, j))
    grad_part = pl.BlockSpec((rows, tile), lambda j: (0, j))
    shapes = part_shapes(rows, 2 * block, places)
    return pl.pallas_call(
        functools.partial(slot_grad_kernel, places),
        grid=(hidden // tile,),
        in_specs=[
            part,
            part,
            grad_part,
            grad_part,
            near,
            near,
            near,
            near,
            whole(x.shape),
        ],
        out_specs=[
            part,
            pl.BlockSpec((2, block, tile), lambda j: (0, 0, j)),
        ]
        + [whole(shape) for shape in shapes],
        out_shape=[
            jax.ShapeDtypeStruct((2, rows, hidden), BF16),
            jax.ShapeDtypeStruct((2, block, hidden), BF16),
        ]
        + [jax.ShapeDtypeStruct(shape, BF16) for shape in shapes],
        scratch_shapes=[pltpu.VMEM((rows, 2 * block), F32)],
        compiler_params=params(),
        cost_estimate=cost(0),
        name="slot_grad",
    )(own, got, own_grad, got_grad, w_gate, w_up, far_gate, far_up, x)


def unslot_kernel(weighted, pick, weight, near, far, other, out):
    half_rows, half = near.shape
    block = half // 2
    replica, expert = lax.axis_index("dp"), lax.axis_index("expert")
    for j in range(4):
        start = pl.multiple_of((replica ^ offset(expert, j)) * block, block)
        own = (near if j < 2 else far)[:, pl.ds((j % 2) * block, block)]
        k = (0, 2, 1, 3)[j]
        rest = other[k // 2, :, pl.ds((k % 2) * block, block)]
        value = plain_dot(pick[:, :half_rows], own) + plain_dot(pick[:, half_rows:], rest)
        if weighted:
            value = weight[:, :1] * value
        out[:, pl.ds(start, block)] = value.astype(BF16)


def unslot(pick, weight, near, far, other, weighted):
    count = pick.shape[0]
    half_rows, half = near.shape
    return pl.pallas_call(
        functools.partial(unslot_kernel, weighted),
        out_shape=jax.ShapeDtypeStruct((count, 2 * half), BF16),
        compiler_params=params(),
        cost_estimate=cost(4),
        name="unslot",
    )(pick, weight, near, far, other)


def swap_chips(parts, chips, *earlier):
    got = list(parts)
    for first in range(0, len(parts), chips):
        for k in range(1, chips):
            got[first + k] = swap_expert(after(parts[first + k], *earlier), 2 * k)
    return got


def send_slots(slots, others, chips, capacity, apart, before_rows, before_near, before_far):
    half = slots.shape[-1]
    other = swap_expert(others, 1)
    far = swap_rows(after(jnp.stack([slots[1], other[1]], axis=0), *before_rows))

    def by_chip(own, rest):
        shape = (chips, 1, capacity, half)
        both = jnp.concatenate([own.reshape(shape), rest.reshape(shape)], axis=1)
        return [both[k].reshape(1, 2 * capacity, half) for k in range(chips)]

    near_parts, far_parts = by_chip(slots[0], other[0]), by_chip(far[0], far[1])
    if apart:
        near_parts = swap_chips(near_parts, chips, *before_near)
        for k in range(1, chips):
            far_parts[k] = after(far_parts[k], near_parts[k])
        return far, near_parts + swap_chips(far_parts, chips, *before_far)
    parts = [jnp.concatenate(pair, axis=0) for pair in zip(near_parts, far_parts)]
    return far, swap_chips(parts, chips, *before_near)


def return_slots(parts, chips, capacity, before_rows, before_core):
    half = parts[0].shape[-1]
    if len(parts) == chips:
        parts = [part[:1] for part in parts] + [part[1:] for part in parts]
    shape = (chips, 2, capacity, half)
    far = swap_rows(after(jnp.concatenate(parts[chips:], axis=0), *before_rows)).reshape(shape)
    near = jnp.concatenate(parts[:chips], axis=0).reshape(shape)
    rows = chips * capacity
    other = jnp.stack([near[:, 1].reshape(rows, half), far[:, 1].reshape(rows, half)], axis=0)
    other = swap_expert(after(other, *before_core), 1)
    return near[:, 0].reshape(rows, half), far[:, 0].reshape(rows, half), other


def body(tokens, cotangent, routes, gate_fixed, w_gate, w_up, w_down):
    tok_count, model_width = tokens.shape
    hidden_width = w_gate.shape[2]
    experts = lax.axis_size("expert")
    chips = experts // 2
    capacity = 3 * tok_count // (2 * experts)
    block = model_width // 4
    tile = 256 if hidden_width % 256 == 0 else hidden_width
    far_gate = swap_weight(w_gate)
    slots, others = make_slots(tokens, routes, gate_fixed, experts, capacity)
    grad_slots, grad_others, pick, weight = make_grads(
        cotangent, routes, gate_fixed, experts, capacity
    )
    far, got_parts = send_slots(
        slots, others, chips, capacity, True, (), (), ()
    )
    far_up = swap_weight(w_up)
    far_down = swap_weight(after(w_down, *(far_up,)))
    grad_far, got_grad_parts = send_slots(
        grad_slots, grad_others, chips, capacity, False, (far_up,), got_parts, got_parts
    )
    if (2 * capacity) % 16 == 0:
        apart = tuple((k,) for k in range(2 * chips))
        paired = tuple((k, k + chips) for k in range(chips))
    else:
        apart = paired = ((0,),)

    def joined(parts):
        if apart != paired:
            return parts
        if len(parts) == chips:
            parts = [part[:1] for part in parts] + [part[1:] for part in parts]
        return [jnp.concatenate(parts, axis=1)]

    def cut(parts):
        if apart != paired:
            return parts
        return jnp.split(parts[0], 2 * chips, axis=1)

    rows, own, send = gate_up_parts(
        joined(got_parts), apart, w_gate, w_up, far_gate, far_up, tile
    )
    got = swap_rows(send)
    grad_rows, own_grad, send_grad = grad_hidden_parts(
        joined(got_grad_parts), paired, after(w_down, *(send,)), far_down, tile
    )
    got_grad = swap_rows(send_grad)

    hidden, far_grad_down, *slot_out = slot_out_parts(
        own, got, w_down, far_down, grad_rows, tile, paired
    )
    out_parts = swap_chips(cut(slot_out), chips)
    sent = [part for k, part in enumerate(out_parts) if k % chips]
    got_down = swap_weight(after(far_grad_down, *(got_grad,)))
    grads, far_grads, *slot_grad = slot_grad_parts(
        own,
        got,
        own_grad,
        after(got_grad, *(hidden,)),
        w_gate,
        w_up,
        far_gate,
        far_up,
        rows,
        tile,
        paired,
    )
    grad_out_parts = cut(slot_grad)
    for k in range(len(grad_out_parts)):
        if k % chips:
            value = after(grad_out_parts[k], out_parts[k % chips])
            grad_out_parts[k] = swap_expert(value, 2 * (k % chips))
    got_far = swap_weight(after(far_grads, *sent[1:2]))

    grad_w_gate = contract_first(rows[:, :block], grads[0]) + got_far[0].astype(F32)
    grad_w_up = contract_first(rows[:, :block], grads[1]) + got_far[1].astype(F32)
    grad_w_down = contract_first(hidden, grad_rows[:, :block]) + got_down.astype(F32)
    grad_w_gate, grad_w_up, grad_w_down = (
        value.astype(BF16)[None] for value in (grad_w_gate, grad_w_up, grad_w_down)
    )

    back = return_slots(out_parts, chips, capacity, (slot_grad[0],), ())
    mixed = unslot(pick, weight, *back, True)
    grad_back = return_slots(grad_out_parts, chips, capacity, (), (mixed,))
    grad_tokens = unslot(pick, weight, *grad_back, False)
    return (
        mixed,
        grad_tokens,
        grad_w_gate,
        grad_w_up,
        grad_w_down,
    )


def solution(mesh):
    return jax.shard_map(
        body,
        mesh=mesh,
        in_specs=(
            P(("dp", "expert"), None),
            P(("dp", "expert"), None),
            P(("dp", "expert"), None),
            P(("dp", "expert"), None),
            P("expert", "dp", None),
            P("expert", "dp", None),
            P("expert", None, "dp"),
        ),
        out_specs=(
            P(("dp", "expert"), None),
            P(("dp", "expert"), None),
            P("expert", "dp", None),
            P("expert", "dp", None),
            P("expert", None, "dp"),
        ),
        check_vma=False,
    )
```
